512 devices in a mesh: batch: 4 (over z_hi, core), patch: 128 (over y, x, z_lo).
Axes of the slice: x: 4, y: 8, z: 8 (z_hi: 2, z_lo: 4; z = z_hi * 4 + z_lo), core: 2. Of those that a mesh axis runs over, the one named last changes fastest.
Arguments:
- latent: bfloat16 [512, 32, 640], P(('batch', 'patch')), parts along dimension 0, may hold values from -45 to 45
- stale_hidden: bfloat16 [16384, 640], P(('batch', 'patch')), parts along dimension 0, may hold values from -5 to 5
- input_proj: bfloat16 [640, 640], replicated, may hold values from -0.25 to 0.25
- query_proj: bfloat16 [640, 640], replicated, may hold values from -20 to 20
- key_proj: bfloat16 [640, 640], replicated, may hold values from -1 to 1
- value_proj: bfloat16 [640, 640], replicated, may hold values from -0.25 to 0.25
- output_proj: bfloat16 [640, 640], replicated, may hold values from -0.25 to 0.25
Outputs:
- level_out: bfloat16 [512, 32, 640], P(('batch', 'patch')), parts along dimension 0
- next_hidden: bfloat16 [16384, 640], P(('batch', 'patch')), parts along dimension 0
The draws below stay inside these ranges and needn't reach their ends.
There are 4 independent parts, one for each index of `batch`. The reference program is written for one: setup_inputs(seed, part) draws one part's arguments, and reference() takes and returns one part's arrays. A program takes and returns all parts, laid end to end along the dimension named above; an argument that names none is the same for every part. Nothing has to cross between parts.
All inputs are finite; a program needn't handle non-finite values.
Results may differ from the reference program's by a relative error of at most 0.0051.
Values may be sent and summed in bfloat16 or wider, within the bound.
No kernel may reach another device: no remote copies, remote signals or barrier semaphores. Data moves between devices by JAX's collectives and lax.ppermute only.
A program may use at most 128 MiB of HBM per device.

```python
import math
import jax
import jax.numpy as jnp
from jax import lax

C = 640
HEADS = 10
HEAD = 64
GROUPS = 32
COLS = 32
BANDS = 128
ROWS = 128
TOK_DEV = 32
TOKENS = 4096


def shared_key_rows(key):
    return jax.random.truncated_normal(key, -5.0, 5.0, (C, C), jnp.float32) * C ** (-0.5)


def draw_latent(key, part):
    key = jax.random.fold_in(key, 3)
    keys = jax.random.split(key, 4)
    row_number = jnp.arange(ROWS, dtype=jnp.float32)
    trend = jnp.exp(jnp.log(3.0) * row_number / max(ROWS - 1, 1))
    noise = jax.random.truncated_normal(keys[0], -4.0, 4.0, (ROWS, COLS, C), jnp.float32)
    row_gain = jnp.exp(jax.random.uniform(keys[1], (ROWS,), jnp.float32, 0.0, jnp.log(3.3)))
    offset = jax.random.uniform(keys[3], (C,), jnp.float32, -0.8, 0.8)
    channel_gain = jnp.exp(jax.random.uniform(keys[2], (C,), jnp.float32, 0.0, jnp.log(3.0)))
    scale = (trend * row_gain)[:, None, None]
    result = scale * (channel_gain * noise + offset) / 3.0
    return result.astype(jnp.bfloat16)


def draw_key_proj(key, part):
    shared = shared_key_rows(key)
    return shared.astype(jnp.bfloat16)


def draw_query_proj(key, part):
    shared = shared_key_rows(key)
    key = jax.random.fold_in(key, 7)
    keys = jax.random.split(key, 2)
    noise = jax.random.truncated_normal(keys[0], -5.0, 5.0, (C, C), jnp.float32) * C ** (-0.5)
    align = jnp.exp(jax.random.uniform(keys[1], (HEADS,), jnp.float32, jnp.log(0.75), jnp.log(1.25)))
    column_gain = jnp.repeat(align, HEAD)
    return (shared * column_gain[None, :] + 0.6 * noise).astype(jnp.bfloat16)


def block_levels(key, dims, cuts, smallest, largest):
    def one(position, shards_of):
        heights = jax.random.uniform(jax.random.fold_in(jax.random.fold_in(key, 6), position), (shards_of,), jnp.float32, smallest / len(cuts), largest / len(cuts))
        return jnp.repeat(jnp.exp(heights), dims[position] // shards_of).reshape((-1,) + (1,) * (len(dims) - position - 1))

    factor_of = one(*cuts[0])
    for cut in cuts[1:]:
        factor_of = factor_of * one(*cut)
    return factor_of


def bell_draw(stream_key, shape, deviation, bound, shards=(), kind=jnp.bfloat16):
    drawn = jax.random.normal(stream_key, shape, jnp.float32) * deviation
    if len(shards) > 0:
        drawn = block_levels(stream_key, shape, shards, -0.22, 0.18) * drawn
    return jnp.clip(drawn, min=-bound, max=bound).astype(kind)


def setup_inputs(seed: int = 0, part: int = 0) -> dict:
    splits = jax.random.split(jax.random.key(seed), 8)
    own_keys = jax.random.split(jax.random.fold_in(splits[7], part), 8)
    return {
        "latent": draw_latent(jax.random.fold_in(jax.random.fold_in(splits[7], part), 71), part),
        "stale_hidden": bell_draw(own_keys[1], (TOKENS, C), 1.0, 5.0, ((0, 128),)),
        "input_proj": bell_draw(splits[2], (C, C), C ** -0.5, 0.25),
        "query_proj": draw_query_proj(jax.random.fold_in(splits[7], 71), part),
        "key_proj": draw_key_proj(jax.random.fold_in(splits[7], 71), part),
        "value_proj": bell_draw(splits[5], (C, C), C ** -0.5, 0.25),
        "output_proj": bell_draw(splits[6], (C, C), C ** -0.5, 0.25),
    }


def group_norm(latent):
    cell_values = latent.astype(jnp.float32).reshape(ROWS, COLS, GROUPS, C // GROUPS)
    center = lax.optimization_barrier(jnp.mean(cell_values, axis=(0, 1, 3), keepdims=True))
    spread = lax.optimization_barrier(jnp.mean(jnp.square(cell_values - center), axis=(0, 1, 3), keepdims=True))
    normed = (cell_values - center) * lax.rsqrt(spread + 1e-06)
    return normed.reshape(ROWS * COLS, C).astype(jnp.bfloat16)

def layer_norm(projected):
    center = lax.optimization_barrier(jnp.mean(projected, axis=-1, keepdims=True))
    spread = lax.optimization_barrier(jnp.mean(jnp.square(projected - center), axis=-1, keepdims=True))
    return ((projected - center) * lax.rsqrt(spread + 1e-05)).astype(jnp.bfloat16)

def reference(latent, stale_hidden, input_proj, query_proj, key_proj, value_proj, output_proj):
    normed = group_norm(latent)
    projected = jnp.dot(normed, input_proj, preferred_element_type=jnp.float32)
    next_hidden = layer_norm(projected)
    queries = jnp.dot(next_hidden, query_proj, preferred_element_type=jnp.float32).astype(jnp.bfloat16)
    fresh_keys = jnp.dot(next_hidden, key_proj, preferred_element_type=jnp.float32).astype(jnp.bfloat16)
    fresh_values = jnp.dot(next_hidden, value_proj, preferred_element_type=jnp.float32).astype(jnp.bfloat16)
    stale_keys = jnp.dot(stale_hidden, key_proj, preferred_element_type=jnp.float32).astype(jnp.bfloat16)
    stale_values = jnp.dot(stale_hidden, value_proj, preferred_element_type=jnp.float32).astype(jnp.bfloat16)

    def attend_band(band_index):
        band_start = (band_index * TOK_DEV).astype(jnp.int32)
        query_rows = lax.dynamic_slice_in_dim(queries, band_start, TOK_DEV, 0)
        band_keys = lax.dynamic_update_slice_in_dim(stale_keys, lax.dynamic_slice_in_dim(fresh_keys, band_start, TOK_DEV, 0), band_start, 0)
        band_values = lax.dynamic_update_slice_in_dim(stale_values, lax.dynamic_slice_in_dim(fresh_values, band_start, TOK_DEV, 0), band_start, 0)
        query_heads = query_rows.astype(jnp.float32).reshape(TOK_DEV, HEADS, HEAD)
        key_heads = band_keys.astype(jnp.float32).reshape(TOKENS, HEADS, HEAD)
        value_heads = band_values.astype(jnp.float32).reshape(TOKENS, HEADS, HEAD)
        scores = jnp.einsum('qhd,khd->hqk', query_heads, key_heads) * (1.0 / math.sqrt(HEAD))
        row_max = lax.optimization_barrier(jnp.max(scores, axis=-1, keepdims=True))
        weights = jnp.exp(scores - row_max)
        row_total = lax.optimization_barrier(jnp.sum(weights, axis=-1, keepdims=True))
        probs = (weights / row_total).astype(jnp.bfloat16)
        attended = jnp.einsum('hqk,khd->qhd', probs.astype(jnp.float32), value_heads)
        return attended.reshape(TOK_DEV, C).astype(jnp.bfloat16)
    attended = lax.map(attend_band, jnp.arange(BANDS, dtype=jnp.int32)).reshape(TOKENS, C)
    mixed_out = jnp.dot(attended, output_proj, preferred_element_type=jnp.float32)
    level_sum = latent.astype(jnp.float32).reshape(TOKENS, C) + projected + mixed_out
    level_out = level_sum.reshape(ROWS, COLS, C).astype(jnp.bfloat16)
    return (level_out, next_hidden)
```

```python
import math

import jax
import jax.numpy as jnp
from jax import lax
from jax.experimental import pallas as pl
from jax.experimental.pallas import tpu as pltpu
from jax.sharding import PartitionSpec as P

C = 640
HEADS = 10
HEAD = 64
GROUP = 20
TOK = 32
BANDS = 128
LANES = 128
SLOT = 32
WIDE = C + LANES
STEP = math.log2(math.e) / math.sqrt(HEAD)
FAR = -1e30

PLACES = [(y, x, z) for y in range(8) for x in range(4) for z in range(4)]


def _groups(key):
    members = {}
    for index, place in enumerate(PLACES):
        members.setdefault(key(*place), []).append(index)
    return [members[k] for k in sorted(members)]


CUBES = _groups(lambda y, x, z: (y // 2, x // 2, z // 2))
CORNERS = _groups(lambda y, x, z: (y % 2, x % 2, z % 2))
NQ = len(CUBES[0])
NK = len(CORNERS[0])
QROWS = NQ * TOK
KROWS = NK * TOK
BF = jnp.bfloat16
F32 = jnp.float32


def _iota(shape, axis):
    return lax.broadcasted_iota(jnp.int32, shape, axis)


def _pieces(value):
    first = value.astype(BF).astype(F32)
    rest = value - first
    second = rest.astype(BF).astype(F32)
    return first, second, rest - second


def stats_kernel(latent_ref, out_ref):
    cells = latent_ref[...].astype(F32).reshape(QROWS, C)
    center = jnp.sum(cells, axis=0, keepdims=True) * (1.0 / QROWS)
    away = jnp.sum(jnp.square(cells - center), axis=0, keepdims=True)
    out_ref[0:1, :] = center
    out_ref[1:2, :] = away


def _group_mean(row, same_group):
    first, second, third = _pieces(row)
    which = _iota((16, C), 0)
    stacked = jnp.where(which == 0, first, jnp.where(which == 1, second, jnp.where(which == 2, third, 0.0)))
    sums = jnp.dot(stacked.astype(BF), same_group, preferred_element_type=F32)
    return jnp.sum(sums, axis=0, keepdims=True) * (1.0 / GROUP)


def _attend(q_pair, k_pair, v_pair, bias):
    rows = q_pair.shape[0]
    left = _iota((rows, LANES), 1) < HEAD
    zero = jnp.zeros_like(q_pair)
    both = jnp.concatenate([jnp.where(left, q_pair, zero), jnp.where(left, zero, q_pair)], axis=0)
    scores = lax.dot_general(both, k_pair, (((1,), (1,)), ((), ())), preferred_element_type=F32)
    if bias is not None:
        scores = scores + bias
    top = jnp.max(scores, axis=1, keepdims=True)
    weights = jnp.exp2((scores - top) * STEP).astype(BF)
    ones = jnp.ones_like(v_pair)
    sums = jnp.dot(weights, jnp.concatenate([v_pair, ones], axis=1), preferred_element_type=F32)
    total = sums[:, LANES:]
    mixed = sums[:, :LANES] / total
    logs = top * STEP + jnp.log2(total)
    return jnp.where(left, mixed[:rows], mixed[rows:]), logs[:rows], logs[rows:]


def _pack_logs(logs):
    first, second, third = _pieces(logs)
    lane = _iota(logs.shape, 1)
    return jnp.where(lane < SLOT, first, jnp.where(lane < 2 * SLOT, second, third)).astype(BF)


def main_kernel(
    place_ref,
    latent_ref,
    stats_ref,
    stale_ref,
    input_ref,
    query_ref,
    key_ref,
    value_ref,
    part_ref,
    own_ref,
    projected_ref,
    hidden_ref,
    projected_all,
    hidden_all,
    queries,
):
    mine = pl.multiple_of(place_ref[0] * TOK, TOK)
    band = place_ref[1]

    stats = stats_ref[...]
    parts_mean = stats[:, 0, :]
    parts_away = stats[:, 1, :]
    mean = jnp.sum(parts_mean, axis=0, keepdims=True) * (1.0 / NK)
    away = jnp.sum(parts_away + float(QROWS) * jnp.square(parts_mean - mean), axis=0, keepdims=True)
    row_group = (_iota((C, C), 0) * 52429) >> 20
    col_group = (_iota((C, C), 1) * 52429) >> 20
    same_group = jnp.where(row_group == col_group, 1.0, 0.0).astype(BF)
    center = _group_mean(mean, same_group)
    spread = _group_mean(away * (1.0 / (QROWS * NK)) + jnp.square(mean - center), same_group)
    gain = lax.rsqrt(spread + 1e-06)
    cells = latent_ref[...].astype(F32).reshape(QROWS, C)
    normed = ((cells - center) * gain).astype(BF)

    projected = jnp.dot(normed, input_ref[...], preferred_element_type=F32)
    projected_all[...] = projected
    row_mean = jnp.mean(projected, axis=1, keepdims=True)
    shifted = projected - row_mean
    row_spread = jnp.mean(jnp.square(shifted), axis=1, keepdims=True)
    hidden = (shifted * lax.rsqrt(row_spread + 1e-05)).astype(BF)
    hidden_all[...] = hidden
    projected_ref[...] = projected_all[pl.ds(mine, TOK), :]
    own_hidden = hidden_all[pl.ds(mine, TOK), :]
    hidden_ref[...] = own_hidden
    queries[...] = jnp.dot(hidden, query_ref[...], preferred_element_type=F32).astype(BF)

    stale = stale_ref[...].reshape(KROWS, C)
    keys = jnp.dot(stale, key_ref[...], preferred_element_type=F32).astype(BF)
    values = jnp.dot(stale, value_ref[...], preferred_element_type=F32).astype(BF)
    fresh_keys = jnp.dot(own_hidden, key_ref[...], preferred_element_type=F32).astype(BF)
    fresh_values = jnp.dot(own_hidden, value_ref[...], preferred_element_type=F32).astype(BF)

    row_band = (_iota((2 * QROWS, KROWS), 0) % QROWS) // TOK
    col_band = _iota((2 * QROWS, KROWS), 1) // TOK
    bias = jnp.where((row_band == place_ref[0]) & (col_band == band), FAR, 0.0).astype(F32)

    lane = _iota((QROWS, LANES), 1) % SLOT
    own_lane = _iota((TOK, LANES), 1) % SLOT
    logs = jnp.zeros((QROWS, LANES), F32)
    own_logs = jnp.zeros((TOK, LANES), F32)
    for pair in range(HEADS // 2):
        cut = slice(pair * LANES, (pair + 1) * LANES)
        mixed, low, high = _attend(queries[:, cut], keys[:, cut], values[:, cut], bias)
        part_ref[:, :, cut] = mixed.astype(BF).reshape(NQ, TOK, LANES)
        logs = jnp.where(lane == 2 * pair, low, jnp.where(lane == 2 * pair + 1, high, logs))
        mixed, low, high = _attend(
            queries[pl.ds(mine, TOK), cut], fresh_keys[:, cut], fresh_values[:, cut], None
        )
        own_ref[:, cut] = mixed.astype(BF)
        own_logs = jnp.where(own_lane == 2 * pair, low, jnp.where(own_lane == 2 * pair + 1, high, own_logs))
    part_ref[:, :, C:] = _pack_logs(logs).reshape(NQ, TOK, LANES)
    own_ref[:, C:] = _pack_logs(own_logs)


def merge_kernel(part_ref, own_ref, projected_ref, latent_ref, output_ref, level_ref):
    slot = _iota((LANES, C), 0)
    head = _iota((LANES, C), 1) // HEAD
    spread = jnp.where((slot % SLOT == head) & (slot < 3 * SLOT), 1.0, 0.0).astype(BF)
    logs = jnp.dot(part_ref[:, :, C:].reshape(QROWS, LANES), spread, preferred_element_type=F32)
    logs = logs.reshape(NQ, TOK, C)
    own_logs = jnp.dot(own_ref[:, C:], spread, preferred_element_type=F32)
    top = jnp.maximum(jnp.max(logs, axis=0), own_logs)
    weight = jnp.exp2(own_logs - top)
    total = weight
    mixed = weight * own_ref[:, :C].astype(F32)
    for index in range(NQ):
        weight = jnp.exp2(logs[index] - top)
        total = total + weight
        mixed = mixed + weight * part_ref[index, :, :C].astype(F32)
    attended = (mixed / total).astype(BF)
    out = jnp.dot(attended, output_ref[...], preferred_element_type=F32)
    level = latent_ref[...].reshape(TOK, C).astype(F32) + projected_ref[...] + out
    level_ref[...] = level.astype(BF).reshape(1, TOK, C)


def _call(kernel, out_shape, n_in, scalar=False, scratch=(), limit=32 * 2**20):
    specs = [pl.BlockSpec(memory_space=pltpu.VMEM)] * n_in
    if scalar:
        specs = [pl.BlockSpec(memory_space=pltpu.SMEM)] + specs[1:]
    several = isinstance(out_shape, tuple)
    whole = pl.BlockSpec(memory_space=pltpu.VMEM)
    return pl.pallas_call(
        kernel,
        out_shape=out_shape,
        in_specs=specs,
        out_specs=(whole,) * len(out_shape) if several else whole,
        scratch_shapes=list(scratch),
        compiler_params=pltpu.CompilerParams(vmem_limit_bytes=limit),
    )


def _share(block, groups):
    copies = jnp.broadcast_to(block[None], (len(groups[0]),) + block.shape)
    return lax.all_to_all(copies, "patch", 0, 0, axis_index_groups=groups)


def on_device(latent, stale_hidden, input_proj, query_proj, key_proj, value_proj, output_proj):
    me = lax.axis_index("patch")
    y, x, z = me // 16, (me // 4) % 4, me % 4
    corner = (y % 2) * 4 + (x % 2) * 2 + z % 2
    cube = (y // 2) * 4 + (x // 2) * 2 + z // 2
    place = jnp.stack([corner, cube]).astype(jnp.int32)

    shape = jax.ShapeDtypeStruct
    stale = _share(stale_hidden, CORNERS)
    latents = _share(latent.reshape(TOK, C), CUBES)
    stats = _call(stats_kernel, shape((2, C), F32), 1)(latents)
    stats = _share(stats, CORNERS)
    parts, own, projected, next_hidden = _call(
        main_kernel,
        (shape((NQ, TOK, WIDE), BF), shape((TOK, WIDE), BF), shape((TOK, C), F32), shape((TOK, C), BF)),
        8,
        scalar=True,
        scratch=(pltpu.VMEM((QROWS, C), F32), pltpu.VMEM((QROWS, C), BF), pltpu.VMEM((QROWS, C), BF)),
    )(place, latents, stats, stale, input_proj, query_proj, key_proj, value_proj)
    parts = lax.all_to_all(parts, "patch", 0, 0, axis_index_groups=CUBES)
    level_out = _call(merge_kernel, shape((1, TOK, C), BF), 5)(parts, own, projected, latent, output_proj)
    return level_out, next_hidden


def solution(mesh):
    rows = P(("batch", "patch"), None)
    return jax.shard_map(
        on_device,
        mesh=mesh,
        in_specs=(P(("batch", "patch"), None, None), rows, P(), P(), P(), P(), P()),
        out_specs=(P(("batch", "patch"), None, None), rows),
        check_vma=False,
    )
```

```python
import math

import jax
import jax.numpy as jnp
from jax import lax
from jax.experimental import pallas as pl
from jax.experimental.pallas import tpu as pltpu
from jax.sharding import PartitionSpec as P

C = 640
HEADS = 10
HEAD = 64
GROUP = 20
TOK = 32
BANDS = 128
LANES = 128
SLOT = 32
WIDE = C + LANES
STATS = TOK * C // LANES
STEP = math.log2(math.e) / math.sqrt(HEAD)
FAR = -1e30

PLACES = [(y, x, z) for y in range(8) for x in range(4) for z in range(4)]


def _groups(key):
    members = {}
    for index, place in enumerate(PLACES):
        members.setdefault(key(*place), []).append(index)
    return [members[k] for k in sorted(members)]


CUBES = _groups(lambda y, x, z: (y // 2, x // 2, z // 2))
CORNERS = _groups(lambda y, x, z: (y % 2, x % 2, z % 2))
NQ = len(CUBES[0])
NK = len(CORNERS[0])
QROWS = NQ * TOK
KROWS = NK * TOK
BF = jnp.bfloat16
F32 = jnp.float32


def _iota(shape, axis):
    return lax.broadcasted_iota(jnp.int32, shape, axis)


def _pieces(value):
    first = value.astype(BF).astype(F32)
    rest = value - first
    second = rest.astype(BF).astype(F32)
    return first, second, rest - second


def _same_group(shape, channel_axis):
    group_axis = 1 - channel_axis
    return jnp.where((_iota(shape, channel_axis) * 52429) >> 20 == _iota(shape, group_axis), 1.0, 0.0).astype(BF)


def _stack_pieces(*rows):
    which = _iota((16, rows[0].shape[1]), 0)
    stacked = jnp.zeros((16, rows[0].shape[1]), F32)
    for index, piece in enumerate(p for row in rows for p in _pieces(row)):
        stacked = jnp.where(which == index, piece, stacked)
    return stacked.astype(BF)


def pack_kernel(latent_ref, stale_ref, out_ref):
    cells = latent_ref[...].astype(F32).reshape(QROWS, C)
    to_group = _same_group((C, LANES), 0)
    to_channel = _same_group((LANES, C), 1)

    def group_sums(row):
        sums = jnp.dot(_stack_pieces(row), to_group, preferred_element_type=F32)
        return jnp.sum(sums, axis=0, keepdims=True)

    center = group_sums(jnp.sum(cells, axis=0, keepdims=True)) * (1.0 / (QROWS * GROUP))
    centers = jnp.dot(_stack_pieces(center), to_channel, preferred_element_type=F32)
    shifted = cells - jnp.sum(centers, axis=0, keepdims=True)
    away = group_sums(jnp.sum(jnp.square(shifted), axis=0, keepdims=True))
    stats = _stack_pieces(center, away)
    for index in range(NK):
        for part in range(C // LANES):
            out_ref[index, part * TOK : (part + 1) * TOK, :] = stale_ref[:, part * LANES : (part + 1) * LANES]
        out_ref[index, STATS:, :] = stats


def _attend(q_pair, k_pair, v_pair, bias):
    rows = q_pair.shape[0]
    left = _iota((rows, LANES), 1) < HEAD
    zero = jnp.zeros_like(q_pair)
    both = jnp.concatenate([jnp.where(left, q_pair, zero), jnp.where(left, zero, q_pair)], axis=0)
    scores = lax.dot_general(both, k_pair, (((1,), (1,)), ((), ())), preferred_element_type=F32)
    if bias is not None:
        scores = scores + bias
    top = jnp.max(scores, axis=1, keepdims=True)
    weights = jnp.exp2((scores - top) * STEP).astype(BF)
    ones = jnp.ones_like(v_pair)
    sums = jnp.dot(weights, jnp.concatenate([v_pair, ones], axis=1), preferred_element_type=F32)
    total = sums[:, LANES:]
    mixed = sums[:, :LANES] / total
    logs = top * STEP + jnp.log2(total)
    return jnp.where(left, mixed[:rows], mixed[rows:]), logs[:rows], logs[rows:]


def _pack_logs(logs):
    first, second, third = _pieces(logs)
    lane = _iota(logs.shape, 1)
    return jnp.where(lane < SLOT, first, jnp.where(lane < 2 * SLOT, second, third)).astype(BF)


def main_kernel(
    place_ref,
    latent_ref,
    block_ref,
    input_ref,
    query_ref,
    key_ref,
    value_ref,
    part_ref,
    own_ref,
    projected_ref,
    hidden_ref,
    projected_all,
    hidden_all,
    queries,
):
    mine = pl.multiple_of(place_ref[0] * TOK, TOK)
    band = place_ref[1]

    stats = block_ref[:, STATS:, :].reshape(NK * 16, LANES)
    target = _iota((2 * NK, NK * 16), 0)
    source = _iota((2 * NK, NK * 16), 1) - (target % NK) * 16 - (target // NK) * 3
    picked = jnp.where((source >= 0) & (source < 3), 1.0, 0.0).astype(BF)
    stats = jnp.dot(picked, stats, preferred_element_type=F32)
    parts_mean, parts_away = stats[:NK], stats[NK:]
    mean = jnp.sum(parts_mean, axis=0, keepdims=True) * (1.0 / NK)
    cell_count = float(QROWS * GROUP)
    away = jnp.sum(parts_away + cell_count * jnp.square(parts_mean - mean), axis=0, keepdims=True)
    gain = lax.rsqrt(away * (1.0 / (cell_count * NK)) + 1e-06)
    spread = jnp.dot(_stack_pieces(mean, gain), _same_group((LANES, C), 1), preferred_element_type=F32)
    which = _iota((16, C), 0)
    center = jnp.sum(jnp.where(which < 3, spread, 0.0), axis=0, keepdims=True)
    gain = jnp.sum(jnp.where(which < 3, 0.0, spread), axis=0, keepdims=True)
    cells = latent_ref[...].astype(F32).reshape(QROWS, C)
    normed = ((cells - center) * gain).astype(BF)

    projected = jnp.dot(normed, input_ref[...], preferred_element_type=F32)
    projected_all[...] = projected
    row_mean = jnp.mean(projected, axis=1, keepdims=True)
    shifted = projected - row_mean
    row_spread = jnp.mean(jnp.square(shifted), axis=1, keepdims=True)
    hidden = (shifted * lax.rsqrt(row_spread + 1e-05)).astype(BF)
    hidden_all[...] = hidden
    projected_ref[...] = projected_all[pl.ds(mine, TOK), :]
    own_hidden = hidden_all[pl.ds(mine, TOK), :]
    hidden_ref[...] = own_hidden
    queries[...] = jnp.dot(hidden, query_ref[...], preferred_element_type=F32).astype(BF)

    stale = jnp.concatenate(
        [block_ref[:, part * TOK : (part + 1) * TOK, :].reshape(KROWS, LANES) for part in range(C // LANES)], axis=1
    )
    keys = jnp.dot(stale, key_ref[...], preferred_element_type=F32).astype(BF)
    values = jnp.dot(stale, value_ref[...], preferred_element_type=F32).astype(BF)
    fresh_keys = jnp.dot(own_hidden, key_ref[...], preferred_element_type=F32).astype(BF)
    fresh_values = jnp.dot(own_hidden, value_ref[...], preferred_element_type=F32).astype(BF)

    row_band = (_iota((2 * QROWS, KROWS), 0) % QROWS) // TOK
    col_band = _iota((2 * QROWS, KROWS), 1) // TOK
    bias = jnp.where((row_band == place_ref[0]) & (col_band == band), FAR, 0.0).astype(F32)

    lane = _iota((QROWS, LANES), 1) % SLOT
    own_lane = _iota((TOK, LANES), 1) % SLOT
    logs = jnp.zeros((QROWS, LANES), F32)
    own_logs = jnp.zeros((TOK, LANES), F32)
    for pair in range(HEADS // 2):
        cut = slice(pair * LANES, (pair + 1) * LANES)
        mixed, low, high = _attend(queries[:, cut], keys[:, cut], values[:, cut], bias)
        part_ref[:, :, cut] = mixed.astype(BF).reshape(NQ, TOK, LANES)
        logs = jnp.where(lane == 2 * pair, low, jnp.where(lane == 2 * pair + 1, high, logs))
        mixed, low, high = _attend(
            queries[pl.ds(mine, TOK), cut], fresh_keys[:, cut], fresh_values[:, cut], None
        )
        own_ref[:, cut] = mixed.astype(BF)
        own_logs = jnp.where(own_lane == 2 * pair, low, jnp.where(own_lane == 2 * pair + 1, high, own_logs))
    part_ref[:, :, C:] = _pack_logs(logs).reshape(NQ, TOK, LANES)
    own_ref[:, C:] = _pack_logs(own_logs)


def merge_kernel(part_ref, own_ref, projected_ref, latent_ref, output_ref, level_ref):
    slot = _iota((LANES, C), 0)
    head = _iota((LANES, C), 1) // HEAD
    spread = jnp.where((slot % SLOT == head) & (slot < 3 * SLOT), 1.0, 0.0).astype(BF)
    logs = jnp.dot(part_ref[:, :, C:].reshape(QROWS, LANES), spread, preferred_element_type=F32)
    logs = logs.reshape(NQ, TOK, C)
    own_logs = jnp.dot(own_ref[:, C:], spread, preferred_element_type=F32)
    top = jnp.maximum(jnp.max(logs, axis=0), own_logs)
    weight = jnp.exp2(own_logs - top)
    total = weight
    mixed = weight * own_ref[:, :C].astype(F32)
    for index in range(NQ):
        weight = jnp.exp2(logs[index] - top)
        total = total + weight
        mixed = mixed + weight * part_ref[index, :, :C].astype(F32)
    attended = (mixed / total).astype(BF)
    out = jnp.dot(attended, output_ref[...], preferred_element_type=F32)
    level = latent_ref[...].reshape(TOK, C).astype(F32) + projected_ref[...] + out
    level_ref[...] = level.astype(BF).reshape(1, TOK, C)


def _call(kernel, out_shape, n_in, scalar=False, scratch=(), limit=32 * 2**20):
    specs = [pl.BlockSpec(memory_space=pltpu.VMEM)] * n_in
    if scalar:
        specs = [pl.BlockSpec(memory_space=pltpu.SMEM)] + specs[1:]
    several = isinstance(out_shape, tuple)
    whole = pl.BlockSpec(memory_space=pltpu.VMEM)
    return pl.pallas_call(
        kernel,
        out_shape=out_shape,
        in_specs=specs,
        out_specs=(whole,) * len(out_shape) if several else whole,
        scratch_shapes=list(scratch),
        compiler_params=pltpu.CompilerParams(vmem_limit_bytes=limit),
    )


def _share(block, groups):
    copies = jnp.broadcast_to(block[None], (len(groups[0]),) + block.shape)
    return lax.all_to_all(copies, "patch", 0, 0, axis_index_groups=groups)


def on_device(latent, stale_hidden, input_proj, query_proj, key_proj, value_proj, output_proj):
    me = lax.axis_index("patch")
    y, x, z = me // 16, (me // 4) % 4, me % 4
    corner = (y % 2) * 4 + (x % 2) * 2 + z % 2
    cube = (y // 2) * 4 + (x // 2) * 2 + z // 2
    place = jnp.stack([corner, cube]).astype(jnp.int32)

    shape = jax.ShapeDtypeStruct
    latents = _share(latent.reshape(TOK, C), CUBES)
    blocks = _call(pack_kernel, shape((NK, STATS + 16, LANES), BF), 2)(latents, stale_hidden)
    blocks = lax.all_to_all(blocks, "patch", 0, 0, axis_index_groups=CORNERS)
    parts, own, projected, next_hidden = _call(
        main_kernel,
        (shape((NQ, TOK, WIDE), BF), shape((TOK, WIDE), BF), shape((TOK, C), F32), shape((TOK, C), BF)),
        7,
        scalar=True,
        scratch=(pltpu.VMEM((QROWS, C), F32), pltpu.VMEM((QROWS, C), BF), pltpu.VMEM((QROWS, C), BF)),
    )(place, latents, blocks, input_proj, query_proj, key_proj, value_proj)
    parts = lax.all_to_all(parts, "patch", 0, 0, axis_index_groups=CUBES)
    level_out = _call(merge_kernel, shape((1, TOK, C), BF), 5)(parts, own, projected, latent, output_proj)
    return level_out, next_hidden


def solution(mesh):
    rows = P(("batch", "patch"), None)
    return jax.shard_map(
        on_device,
        mesh=mesh,
        in_specs=(P(("batch", "patch"), None, None), rows, P(), P(), P(), P(), P()),
        out_specs=(P(("batch", "patch"), None, None), rows),
        check_vma=False,
    )
```

```python
import math

import jax
import jax.numpy as jnp
from jax import lax
from jax.experimental import pallas as pl
from jax.experimental.pallas import tpu as pltpu
from jax.sharding import PartitionSpec as P

C = 640
HEADS = 10
HEAD = 64
GROUP = 20
TOK = 32
BANDS = 128
LANES = 128
SLOT = 32
WIDE = C + LANES
STATS = TOK * C // LANES
STEP = math.log2(math.e) / math.sqrt(HEAD)
FAR = -1e30

PLACES = [(y, x, z) for y in range(8) for x in range(4) for z in range(4)]


def _groups(key):
    members = {}
    for index, place in enumerate(PLACES):
        members.setdefault(key(*place), []).append(index)
    return [members[k] for k in sorted(members)]


BRICKS = _groups(lambda y, x, z: (y // 2, z // 2))
SEATS = _groups(lambda y, x, z: (y % 2, x, z % 2))
NQ = len(BRICKS[0])
NK = len(SEATS[0])
QROWS = NQ * TOK
KROWS = NK * TOK
BF = jnp.bfloat16
F32 = jnp.float32


def _iota(shape, axis):
    return lax.broadcasted_iota(jnp.int32, shape, axis)


def _pieces(value):
    first = value.astype(BF).astype(F32)
    rest = value - first
    second = rest.astype(BF).astype(F32)
    return first, second, rest - second


def _same_group(shape, channel_axis):
    group_axis = 1 - channel_axis
    return jnp.where((_iota(shape, channel_axis) * 52429) >> 20 == _iota(shape, group_axis), 1.0, 0.0).astype(BF)


def _stack_pieces(*rows):
    which = _iota((16, rows[0].shape[1]), 0)
    stacked = jnp.zeros((16, rows[0].shape[1]), F32)
    for index, piece in enumerate(p for row in rows for p in _pieces(row)):
        stacked = jnp.where(which == index, piece, stacked)
    return stacked.astype(BF)


def pack_kernel(latent_ref, stale_ref, out_ref):
    cells = latent_ref[...].astype(F32).reshape(QROWS, C)
    to_group = _same_group((C, LANES), 0)
    to_channel = _same_group((LANES, C), 1)

    def group_sums(row):
        sums = jnp.dot(_stack_pieces(row), to_group, preferred_element_type=F32)
        return jnp.sum(sums, axis=0, keepdims=True)

    center = group_sums(jnp.sum(cells, axis=0, keepdims=True)) * (1.0 / (QROWS * GROUP))
    centers = jnp.dot(_stack_pieces(center), to_channel, preferred_element_type=F32)
    shifted = cells - jnp.sum(centers, axis=0, keepdims=True)
    away = group_sums(jnp.sum(jnp.square(shifted), axis=0, keepdims=True))
    stats = _stack_pieces(center, away)
    for index in range(NK):
        for part in range(C // LANES):
            out_ref[index, part * TOK : (part + 1) * TOK, :] = stale_ref[:, part * LANES : (part + 1) * LANES]
        out_ref[index, STATS:, :] = stats


def _attend(q_pair, k_pair, v_pair, bias):
    rows = q_pair.shape[0]
    left = _iota((rows, LANES), 1) < HEAD
    zero = jnp.zeros_like(q_pair)
    both = jnp.concatenate([jnp.where(left, q_pair, zero), jnp.where(left, zero, q_pair)], axis=0)
    scores = lax.dot_general(both, k_pair, (((1,), (1,)), ((), ())), preferred_element_type=F32)
    if bias is not None:
        scores = scores + bias
    top = jnp.max(scores, axis=1, keepdims=True)
    weights = jnp.exp2((scores - top) * STEP).astype(BF)
    ones = jnp.ones_like(v_pair)
    sums = jnp.dot(weights, jnp.concatenate([v_pair, ones], axis=1), preferred_element_type=F32)
    total = sums[:, LANES:]
    mixed = sums[:, :LANES] / total
    logs = top * STEP + jnp.log2(total)
    return jnp.where(left, mixed[:rows], mixed[rows:]), logs[:rows], logs[rows:]


def _pack_logs(logs):
    first, second, third = _pieces(logs)
    lane = _iota(logs.shape, 1)
    return jnp.where(lane < SLOT, first, jnp.where(lane < 2 * SLOT, second, third)).astype(BF)


def main_kernel(
    place_ref,
    latent_ref,
    block_ref,
    input_ref,
    query_ref,
    key_ref,
    value_ref,
    part_ref,
    own_ref,
    projected_ref,
    hidden_ref,
    projected_all,
    hidden_all,
    queries,
):
    mine = pl.multiple_of(place_ref[0] * TOK, TOK)
    band = place_ref[1]

    stats = block_ref[:, STATS:, :].reshape(NK * 16, LANES)
    target = _iota((2 * NK, NK * 16), 0)
    source = _iota((2 * NK, NK * 16), 1) - (target % NK) * 16 - (target // NK) * 3
    picked = jnp.where((source >= 0) & (source < 3), 1.0, 0.0).astype(BF)
    stats = jnp.dot(picked, stats, preferred_element_type=F32)
    parts_mean, parts_away = stats[:NK], stats[NK:]
    mean = jnp.sum(parts_mean, axis=0, keepdims=True) * (1.0 / NK)
    cell_count = float(QROWS * GROUP)
    away = jnp.sum(parts_away + cell_count * jnp.square(parts_mean - mean), axis=0, keepdims=True)
    gain = lax.rsqrt(away * (1.0 / (cell_count * NK)) + 1e-06)
    spread = jnp.dot(_stack_pieces(mean, gain), _same_group((LANES, C), 1), preferred_element_type=F32)
    which = _iota((16, C), 0)
    center = jnp.sum(jnp.where(which < 3, spread, 0.0), axis=0, keepdims=True)
    gain = jnp.sum(jnp.where(which < 3, 0.0, spread), axis=0, keepdims=True)
    cells = latent_ref[...].astype(F32).reshape(QROWS, C)
    normed = ((cells - center) * gain).astype(BF)

    projected = jnp.dot(normed, input_ref[...], preferred_element_type=F32)
    projected_all[...] = projected
    row_mean = jnp.mean(projected, axis=1, keepdims=True)
    shifted = projected - row_mean
    row_spread = jnp.mean(jnp.square(shifted), axis=1, keepdims=True)
    hidden = (shifted * lax.rsqrt(row_spread + 1e-05)).astype(BF)
    hidden_all[...] = hidden
    projected_ref[...] = projected_all[pl.ds(mine, TOK), :]
    own_hidden = hidden_all[pl.ds(mine, TOK), :]
    hidden_ref[...] = own_hidden
    queries[...] = jnp.dot(hidden, query_ref[...], preferred_element_type=F32).astype(BF)

    stale = jnp.concatenate(
        [block_ref[:, part * TOK : (part + 1) * TOK, :].reshape(KROWS, LANES) for part in range(C // LANES)], axis=1
    )
    keys = jnp.dot(stale, key_ref[...], preferred_element_type=F32).astype(BF)
    values = jnp.dot(stale, value_ref[...], preferred_element_type=F32).astype(BF)
    fresh_keys = jnp.dot(own_hidden, key_ref[...], preferred_element_type=F32).astype(BF)
    fresh_values = jnp.dot(own_hidden, value_ref[...], preferred_element_type=F32).astype(BF)

    row_band = (_iota((2 * QROWS, KROWS), 0) % QROWS) // TOK
    col_band = _iota((2 * QROWS, KROWS), 1) // TOK
    bias = jnp.where((row_band == place_ref[0]) & (col_band == band), FAR, 0.0).astype(F32)

    lane = _iota((QROWS, LANES), 1) % SLOT
    own_lane = _iota((TOK, LANES), 1) % SLOT
    logs = jnp.zeros((QROWS, LANES), F32)
    own_logs = jnp.zeros((TOK, LANES), F32)
    for pair in range(HEADS // 2):
        cut = slice(pair * LANES, (pair + 1) * LANES)
        mixed, low, high = _attend(queries[:, cut], keys[:, cut], values[:, cut], bias)
        part_ref[:, :, cut] = mixed.astype(BF).reshape(NQ, TOK, LANES)
        logs = jnp.where(lane == 2 * pair, low, jnp.where(lane == 2 * pair + 1, high, logs))
        mixed, low, high = _attend(
            queries[pl.ds(mine, TOK), cut], fresh_keys[:, cut], fresh_values[:, cut], None
        )
        own_ref[:, cut] = mixed.astype(BF)
        own_logs = jnp.where(own_lane == 2 * pair, low, jnp.where(own_lane == 2 * pair + 1, high, own_logs))
    part_ref[:, :, C:] = _pack_logs(logs).reshape(NQ, TOK, LANES)
    own_ref[:, C:] = _pack_logs(own_logs)


def merge_kernel(part_ref, own_ref, projected_ref, latent_ref, output_ref, level_ref):
    slot = _iota((LANES, C), 0)
    head = _iota((LANES, C), 1) // HEAD
    spread = jnp.where((slot % SLOT == head) & (slot < 3 * SLOT), 1.0, 0.0).astype(BF)
    logs = jnp.dot(part_ref[:, :, C:].reshape(QROWS, LANES), spread, preferred_element_type=F32)
    logs = logs.reshape(NQ, TOK, C)
    own_logs = jnp.dot(own_ref[:, C:], spread, preferred_element_type=F32)
    top = jnp.maximum(jnp.max(logs, axis=0), own_logs)
    weight = jnp.exp2(own_logs - top)
    total = weight
    mixed = weight * own_ref[:, :C].astype(F32)
    for index in range(NQ):
        weight = jnp.exp2(logs[index] - top)
        total = total + weight
        mixed = mixed + weight * part_ref[index, :, :C].astype(F32)
    attended = (mixed / total).astype(BF)
    out = jnp.dot(attended, output_ref[...], preferred_element_type=F32)
    level = latent_ref[...].reshape(TOK, C).astype(F32) + projected_ref[...] + out
    level_ref[...] = level.astype(BF).reshape(1, TOK, C)


def _call(kernel, out_shape, n_in, scalar=False, scratch=(), limit=16 * 2**20):
    specs = [pl.BlockSpec(memory_space=pltpu.VMEM)] * n_in
    if scalar:
        specs = [pl.BlockSpec(memory_space=pltpu.SMEM)] + specs[1:]
    several = isinstance(out_shape, tuple)
    whole = pl.BlockSpec(memory_space=pltpu.VMEM)
    return pl.pallas_call(
        kernel,
        out_shape=out_shape,
        in_specs=specs,
        out_specs=(whole,) * len(out_shape) if several else whole,
        scratch_shapes=list(scratch),
        compiler_params=pltpu.CompilerParams(vmem_limit_bytes=limit),
    )


def _share(block, groups):
    copies = jnp.broadcast_to(block[None], (len(groups[0]),) + block.shape)
    return lax.all_to_all(copies, "patch", 0, 0, axis_index_groups=groups)


def on_device(latent, stale_hidden, input_proj, query_proj, key_proj, value_proj, output_proj):
    me = lax.axis_index("patch")
    y, x, z = me // 16, (me // 4) % 4, me % 4
    place = jnp.stack([(y % 2) * 8 + x * 2 + z % 2, (y // 2) * 2 + z // 2]).astype(jnp.int32)

    shape = jax.ShapeDtypeStruct
    latents = _share(latent.reshape(TOK, C), BRICKS)
    blocks = _call(pack_kernel, shape((NK, STATS + 16, LANES), BF), 2)(latents, stale_hidden)
    blocks = lax.all_to_all(blocks, "patch", 0, 0, axis_index_groups=SEATS)
    parts, own, projected, next_hidden = _call(
        main_kernel,
        (shape((NQ, TOK, WIDE), BF), shape((TOK, WIDE), BF), shape((TOK, C), F32), shape((TOK, C), BF)),
        7,
        scalar=True,
        scratch=(pltpu.VMEM((QROWS, C), F32), pltpu.VMEM((QROWS, C), BF), pltpu.VMEM((QROWS, C), BF)),
    )(place, latents, blocks, input_proj, query_proj, key_proj, value_proj)
    parts = lax.all_to_all(parts, "patch", 0, 0, axis_index_groups=BRICKS)
    level_out = _call(merge_kernel, shape((1, TOK, C), BF), 5)(parts, own, projected, latent, output_proj)
    return level_out, next_hidden


def solution(mesh):
    rows = P(("batch", "patch"), None)
    return jax.shard_map(
        on_device,
        mesh=mesh,
        in_specs=(P(("batch", "patch"), None, None), rows, P(), P(), P(), P(), P()),
        out_specs=(P(("batch", "patch"), None, None), rows),
        check_vma=False,
    )
```

```python
import math

import jax
import jax.numpy as jnp
from jax import lax
from jax.experimental import pallas as pl
from jax.experimental.pallas import tpu as pltpu
from jax.sharding import PartitionSpec as P

C = 640
HEADS = 10
HEAD = 64
GROUP = 20
TOK = 32
BANDS = 128
LANES = 128
SLOT = 32
WIDE = C + LANES
STATS = TOK * C // LANES
STEP = math.log2(math.e) / math.sqrt(HEAD)
FAR = -1e30

PLACES = [(y, x, z) for y in range(8) for x in range(4) for z in range(4)]


def _groups(key):
    members = {}
    for index, place in enumerate(PLACES):
        members.setdefault(key(*place), []).append(index)
    return [members[k] for k in sorted(members)]


BRICKS = _groups(lambda y, x, z: (y // 2, z // 2))
SEATS = _groups(lambda y, x, z: (y % 2, x, z % 2))
NQ = len(BRICKS[0])
NK = len(SEATS[0])
QROWS = NQ * TOK
KROWS = NK * TOK
BF = jnp.bfloat16
F32 = jnp.float32


def _iota(shape, axis):
    return lax.broadcasted_iota(jnp.int32, shape, axis)


def _pieces(value):
    first = value.astype(BF).astype(F32)
    rest = value - first
    second = rest.astype(BF).astype(F32)
    return first, second, rest - second


def _same_group(shape, channel_axis):
    group_axis = 1 - channel_axis
    return jnp.where((_iota(shape, channel_axis) * 52429) >> 20 == _iota(shape, group_axis), 1.0, 0.0).astype(BF)


def _stack_pieces(*rows):
    which = _iota((16, rows[0].shape[1]), 0)
    stacked = jnp.zeros((16, rows[0].shape[1]), F32)
    for index, piece in enumerate(p for row in rows for p in _pieces(row)):
        stacked = jnp.where(which == index, piece, stacked)
    return stacked.astype(BF)


def pack_kernel(latent_ref, stale_ref, out_ref):
    cells = latent_ref[...].astype(F32).reshape(QROWS, C)
    to_group = _same_group((C, LANES), 0)
    to_channel = _same_group((LANES, C), 1)

    def group_sums(row):
        sums = jnp.dot(_stack_pieces(row), to_group, preferred_element_type=F32)
        return jnp.sum(sums, axis=0, keepdims=True)

    center = group_sums(jnp.sum(cells, axis=0, keepdims=True)) * (1.0 / (QROWS * GROUP))
    centers = jnp.dot(_stack_pieces(center), to_channel, preferred_element_type=F32)
    shifted = cells - jnp.sum(centers, axis=0, keepdims=True)
    away = group_sums(jnp.sum(jnp.square(shifted), axis=0, keepdims=True))
    stats = _stack_pieces(center, away)
    for index in range(NK):
        for part in range(C // LANES):
            out_ref[index, part * TOK : (part + 1) * TOK, :] = stale_ref[:, part * LANES : (part + 1) * LANES]
        out_ref[index, STATS:, :] = stats


def _attend(q_pair, k_pair, v_pair, bias):
    rows = q_pair.shape[0]
    left = _iota((rows, LANES), 1) < HEAD
    zero = jnp.zeros_like(q_pair)
    both = jnp.concatenate([jnp.where(left, q_pair, zero), jnp.where(left, zero, q_pair)], axis=0)
    scores = lax.dot_general(both, k_pair, (((1,), (1,)), ((), ())), preferred_element_type=F32)
    if bias is not None:
        scores = scores + bias
    top = jnp.max(scores, axis=1, keepdims=True)
    weights = jnp.exp2((scores - top) * STEP).astype(BF)
    ones = jnp.ones_like(v_pair)
    sums = jnp.dot(weights, jnp.concatenate([v_pair, ones], axis=1), preferred_element_type=F32)
    total = sums[:, LANES:]
    mixed = sums[:, :LANES] / total
    logs = top * STEP + jnp.log2(total)
    return jnp.where(left, mixed[:rows], mixed[rows:]), logs[:rows], logs[rows:]


def _pack_logs(logs):
    first, second, third = _pieces(logs)
    lane = _iota(logs.shape, 1)
    return jnp.where(lane < SLOT, first, jnp.where(lane < 2 * SLOT, second, third)).astype(BF)


def _seat():
    me = lax.axis_index("patch")
    return ((me >> 4) & 1) * 8 + ((me >> 2) & 3) * 2 + (me & 1)


def _brick():
    me = lax.axis_index("patch")
    return (me >> 5) * 2 + ((me >> 1) & 1)


def query_kernel(
    latent_ref, block_ref, input_ref, query_ref, queries_ref, own_queries_ref, projected_ref, hidden_ref, projected_all, hidden_all
):
    mine = pl.multiple_of(_seat() * TOK, TOK)

    stats = block_ref[:, STATS:, :].reshape(NK * 16, LANES)
    target = _iota((2 * NK, NK * 16), 0)
    source = _iota((2 * NK, NK * 16), 1) - (target % NK) * 16 - (target // NK) * 3
    picked = jnp.where((source >= 0) & (source < 3), 1.0, 0.0).astype(BF)
    stats = jnp.dot(picked, stats, preferred_element_type=F32)
    parts_mean, parts_away = stats[:NK], stats[NK:]
    mean = jnp.sum(parts_mean, axis=0, keepdims=True) * (1.0 / NK)
    cell_count = float(QROWS * GROUP)
    away = jnp.sum(parts_away + cell_count * jnp.square(parts_mean - mean), axis=0, keepdims=True)
    gain = lax.rsqrt(away * (1.0 / (cell_count * NK)) + 1e-06)
    spread = jnp.dot(_stack_pieces(mean, gain), _same_group((LANES, C), 1), preferred_element_type=F32)
    which = _iota((16, C), 0)
    center = jnp.sum(jnp.where(which < 3, spread, 0.0), axis=0, keepdims=True)
    gain = jnp.sum(jnp.where(which < 3, 0.0, spread), axis=0, keepdims=True)
    cells = latent_ref[...].astype(F32).reshape(QROWS, C)
    normed = ((cells - center) * gain).astype(BF)

    projected = jnp.dot(normed, input_ref[...], preferred_element_type=F32)
    projected_all[...] = projected
    row_mean = jnp.mean(projected, axis=1, keepdims=True)
    shifted = projected - row_mean
    row_spread = jnp.mean(jnp.square(shifted), axis=1, keepdims=True)
    hidden = (shifted * lax.rsqrt(row_spread + 1e-05)).astype(BF)
    hidden_all[...] = hidden
    queries_ref[...] = jnp.dot(hidden, query_ref[...], preferred_element_type=F32).astype(BF)
    projected_ref[...] = projected_all[pl.ds(mine, TOK), :]
    hidden_ref[...] = hidden_all[pl.ds(mine, TOK), :]
    own_queries_ref[...] = queries_ref[pl.ds(mine, TOK), :]


def attend_kernel(queries_ref, own_queries_ref, hidden_ref, block_ref, key_ref, value_ref, part_ref, own_ref):
    strips = [block_ref[:, part * TOK : (part + 1) * TOK, :].reshape(KROWS, LANES) for part in range(C // LANES)]
    both_hidden = jnp.concatenate([jnp.concatenate(strips, axis=1), hidden_ref[...]], axis=0)
    both_keys = jnp.dot(both_hidden, key_ref[...], preferred_element_type=F32).astype(BF)
    both_values = jnp.dot(both_hidden, value_ref[...], preferred_element_type=F32).astype(BF)
    keys, fresh_keys = both_keys[:KROWS], both_keys[KROWS:]
    values, fresh_values = both_values[:KROWS], both_values[KROWS:]

    row_band = (_iota((2 * QROWS, KROWS), 0) % QROWS) // TOK
    col_band = _iota((2 * QROWS, KROWS), 1) // TOK
    bias = jnp.where((row_band == _seat()) & (col_band == _brick()), FAR, 0.0).astype(F32)

    lane = _iota((QROWS, LANES), 1) % SLOT
    own_lane = _iota((TOK, LANES), 1) % SLOT
    logs = jnp.zeros((QROWS, LANES), F32)
    own_logs = jnp.zeros((TOK, LANES), F32)
    for pair in range(HEADS // 2):
        cut = slice(pair * LANES, (pair + 1) * LANES)
        mixed, low, high = _attend(queries_ref[:, cut], keys[:, cut], values[:, cut], bias)
        part_ref[:, :, cut] = mixed.astype(BF).reshape(NQ, TOK, LANES)
        logs = jnp.where(lane == 2 * pair, low, jnp.where(lane == 2 * pair + 1, high, logs))
        mixed, low, high = _attend(
            own_queries_ref[:, cut], fresh_keys[:, cut], fresh_values[:, cut], None
        )
        own_ref[:, cut] = mixed.astype(BF)
        own_logs = jnp.where(own_lane == 2 * pair, low, jnp.where(own_lane == 2 * pair + 1, high, own_logs))
    part_ref[:, :, C:] = _pack_logs(logs).reshape(NQ, TOK, LANES)
    own_ref[:, C:] = _pack_logs(own_logs)


def merge_kernel(part_ref, own_ref, projected_ref, hidden_ref, latent_ref, output_ref, level_ref, next_ref):
    next_ref[...] = hidden_ref[...]
    slot = _iota((LANES, C), 0)
    head = _iota((LANES, C), 1) // HEAD
    spread = jnp.where((slot % SLOT == head) & (slot < 3 * SLOT), 1.0, 0.0).astype(BF)
    logs = jnp.dot(part_ref[:, :, C:].reshape(QROWS, LANES), spread, preferred_element_type=F32)
    logs = logs.reshape(NQ, TOK, C)
    own_logs = jnp.dot(own_ref[:, C:], spread, preferred_element_type=F32)
    top = jnp.maximum(jnp.max(logs, axis=0), own_logs)
    weight = jnp.exp2(own_logs - top)
    total = weight
    mixed = weight * own_ref[:, :C].astype(F32)
    for index in range(NQ):
        weight = jnp.exp2(logs[index] - top)
        total = total + weight
        mixed = mixed + weight * part_ref[index, :, :C].astype(F32)
    attended = (mixed / total).astype(BF)
    out = jnp.dot(attended, output_ref[...], preferred_element_type=F32)
    level = latent_ref[...].reshape(TOK, C).astype(F32) + projected_ref[...] + out
    level_ref[...] = level.astype(BF).reshape(1, TOK, C)


def _call(kernel, out_shape, n_in, scratch=(), limit=16 * 2**20):
    specs = [pl.BlockSpec(memory_space=pltpu.VMEM)] * n_in
    several = isinstance(out_shape, tuple)
    whole = pl.BlockSpec(memory_space=pltpu.VMEM)
    return pl.pallas_call(
        kernel,
        out_shape=out_shape,
        in_specs=specs,
        out_specs=(whole,) * len(out_shape) if several else whole,
        scratch_shapes=list(scratch),
        compiler_params=pltpu.CompilerParams(vmem_limit_bytes=limit),
    )


def _share(block, groups):
    copies = jnp.broadcast_to(block[None], (len(groups[0]),) + block.shape)
    return lax.all_to_all(copies, "patch", 0, 0, axis_index_groups=groups)


def on_device(latent, stale_hidden, input_proj, query_proj, key_proj, value_proj, output_proj):
    shape = jax.ShapeDtypeStruct
    latents = _share(latent.reshape(TOK, C), BRICKS)
    blocks = _call(pack_kernel, shape((NK, STATS + 16, LANES), BF), 2)(latents, stale_hidden)
    blocks = lax.all_to_all(blocks, "patch", 0, 0, axis_index_groups=SEATS)
    queries, own_queries, projected, hidden = _call(
        query_kernel,
        (shape((QROWS, C), BF), shape((TOK, C), BF), shape((TOK, C), F32), shape((TOK, C), BF)),
        4,
        scratch=(pltpu.VMEM((QROWS, C), F32), pltpu.VMEM((QROWS, C), BF)),
    )(latents, blocks, input_proj, query_proj)
    parts, own = _call(attend_kernel, (shape((NQ, TOK, WIDE), BF), shape((TOK, WIDE), BF)), 6)(
        queries, own_queries, hidden, blocks, key_proj, value_proj
    )
    parts = lax.all_to_all(parts, "patch", 0, 0, axis_index_groups=BRICKS)
    return _call(merge_kernel, (shape((1, TOK, C), BF), shape((TOK, C), BF)), 6)(
        parts, own, projected, hidden, latent, output_proj
    )


def solution(mesh):
    rows = P(("batch", "patch"), None)
    return jax.shard_map(
        on_device,
        mesh=mesh,
        in_specs=(P(("batch", "patch"), None, None), rows, P(), P(), P(), P(), P()),
        out_specs=(P(("batch", "patch"), None, None), rows),
        check_vma=False,
    )
```

```python
import math

import jax
import jax.numpy as jnp
from jax import lax
from jax.experimental import pallas as pl
from jax.experimental.pallas import tpu as pltpu
from jax.sharding import PartitionSpec as P

C = 640
HEADS = 10
HEAD = 64
GROUP = 20
TOK = 32
BANDS = 128
LANES = 128
SLOT = 32
WIDE = C + LANES
STATS = TOK * C // LANES
STEP = math.log2(math.e) / math.sqrt(HEAD)
FAR = -1e30

PLACES = [(y, x, z) for y in range(8) for x in range(4) for z in range(4)]


def _groups(key):
    members = {}
    for index, place in enumerate(PLACES):
        members.setdefault(key(*place), []).append(index)
    return [members[k] for k in sorted(members)]


BRICKS = _groups(lambda y, x, z: (y // 2, x // 2, z // 2))
SEATS = _groups(lambda y, x, z: (y % 2, x % 2, z % 2))
NQ = len(BRICKS[0])
NK = len(SEATS[0])
QROWS = NQ * TOK
KROWS = NK * TOK
BF = jnp.bfloat16
F32 = jnp.float32


def _iota(shape, axis):
    return lax.broadcasted_iota(jnp.int32, shape, axis)


def _pieces(value):
    first = value.astype(BF).astype(F32)
    rest = value - first
    second = rest.astype(BF).astype(F32)
    return first, second, rest - second


def _same_group(shape, channel_axis):
    group_axis = 1 - channel_axis
    return jnp.where((_iota(shape, channel_axis) * 52429) >> 20 == _iota(shape, group_axis), 1.0, 0.0).astype(BF)


def _stack_pieces(*rows):
    which = _iota((16, rows[0].shape[1]), 0)
    stacked = jnp.zeros((16, rows[0].shape[1]), F32)
    for index, piece in enumerate(p for row in rows for p in _pieces(row)):
        stacked = jnp.where(which == index, piece, stacked)
    return stacked.astype(BF)


def pack_kernel(latent_ref, stale_ref, out_ref):
    cells = latent_ref[...].astype(F32).reshape(QROWS, C)
    to_group = _same_group((C, LANES), 0)
    to_channel = _same_group((LANES, C), 1)

    def group_sums(row):
        sums = jnp.dot(_stack_pieces(row), to_group, preferred_element_type=F32)
        return jnp.sum(sums, axis=0, keepdims=True)

    center = group_sums(jnp.sum(cells, axis=0, keepdims=True)) * (1.0 / (QROWS * GROUP))
    centers = jnp.dot(_stack_pieces(center), to_channel, preferred_element_type=F32)
    shifted = cells - jnp.sum(centers, axis=0, keepdims=True)
    away = group_sums(jnp.sum(jnp.square(shifted), axis=0, keepdims=True))
    stats = _stack_pieces(center, away)
    for index in range(NK):
        for part in range(C // LANES):
            out_ref[index, part * TOK : (part + 1) * TOK, :] = stale_ref[:, part * LANES : (part + 1) * LANES]
        out_ref[index, STATS:, :] = stats


def _attend(q_pair, k_pair, v_pair, bias):
    rows = q_pair.shape[0]
    left = _iota((rows, LANES), 1) < HEAD
    zero = jnp.zeros_like(q_pair)
    both = jnp.concatenate([jnp.where(left, q_pair, zero), jnp.where(left, zero, q_pair)], axis=0)
    scores = lax.dot_general(both, k_pair, (((1,), (1,)), ((), ())), preferred_element_type=F32)
    if bias is not None:
        scores = scores + bias
    top = jnp.max(scores, axis=1, keepdims=True)
    weights = jnp.exp2((scores - top) * STEP).astype(BF)
    ones = jnp.ones_like(v_pair)
    sums = jnp.dot(weights, jnp.concatenate([v_pair, ones], axis=1), preferred_element_type=F32)
    total = sums[:, LANES:]
    mixed = sums[:, :LANES] / total
    logs = top * STEP + jnp.log2(total)
    return jnp.where(left, mixed[:rows], mixed[rows:]), logs[:rows], logs[rows:]


def _pack_logs(logs):
    first, second, third = _pieces(logs)
    lane = _iota(logs.shape, 1)
    return jnp.where(lane < SLOT, first, jnp.where(lane < 2 * SLOT, second, third)).astype(BF)


def _seat():
    me = lax.axis_index("patch")
    return ((me >> 4) & 1) * 4 + ((me >> 2) & 1) * 2 + (me & 1)


def _brick():
    me = lax.axis_index("patch")
    return (me >> 5) * 4 + ((me >> 3) & 1) * 2 + ((me >> 1) & 1)


def query_kernel(
    latent_ref, block_ref, input_ref, query_ref, queries_ref, own_queries_ref, projected_ref, hidden_ref, projected_all, hidden_all
):
    mine = pl.multiple_of(_seat() * TOK, TOK)

    stats = block_ref[:, STATS:, :].reshape(NK * 16, LANES)
    target = _iota((2 * NK, NK * 16), 0)
    source = _iota((2 * NK, NK * 16), 1) - (target % NK) * 16 - (target // NK) * 3
    picked = jnp.where((source >= 0) & (source < 3), 1.0, 0.0).astype(BF)
    stats = jnp.dot(picked, stats, preferred_element_type=F32)
    parts_mean, parts_away = stats[:NK], stats[NK:]
    mean = jnp.sum(parts_mean, axis=0, keepdims=True) * (1.0 / NK)
    cell_count = float(QROWS * GROUP)
    away = jnp.sum(parts_away + cell_count * jnp.square(parts_mean - mean), axis=0, keepdims=True)
    gain = lax.rsqrt(away * (1.0 / (cell_count * NK)) + 1e-06)
    spread = jnp.dot(_stack_pieces(mean, gain), _same_group((LANES, C), 1), preferred_element_type=F32)
    which = _iota((16, C), 0)
    center = jnp.sum(jnp.where(which < 3, spread, 0.0), axis=0, keepdims=True)
    gain = jnp.sum(jnp.where(which < 3, 0.0, spread), axis=0, keepdims=True)
    cells = latent_ref[...].astype(F32).reshape(QROWS, C)
    normed = ((cells - center) * gain).astype(BF)

    projected = jnp.dot(normed, input_ref[...], preferred_element_type=F32)
    projected_all[...] = projected
    row_mean = jnp.mean(projected, axis=1, keepdims=True)
    shifted = projected - row_mean
    row_spread = jnp.mean(jnp.square(shifted), axis=1, keepdims=True)
    hidden = (shifted * lax.rsqrt(row_spread + 1e-05)).astype(BF)
    hidden_all[...] = hidden
    queries_ref[...] = jnp.dot(hidden, query_ref[...], preferred_element_type=F32).astype(BF)
    projected_ref[...] = projected_all[pl.ds(mine, TOK), :]
    hidden_ref[...] = hidden_all[pl.ds(mine, TOK), :]
    own_queries_ref[...] = queries_ref[pl.ds(mine, TOK), :]


def attend_kernel(queries_ref, own_queries_ref, hidden_ref, block_ref, key_ref, value_ref, part_ref, own_ref):
    strips = [block_ref[:, part * TOK : (part + 1) * TOK, :].reshape(KROWS, LANES) for part in range(C // LANES)]
    both_hidden = jnp.concatenate([jnp.concatenate(strips, axis=1), hidden_ref[...]], axis=0)
    both_keys = jnp.dot(both_hidden, key_ref[...], preferred_element_type=F32).astype(BF)
    both_values = jnp.dot(both_hidden, value_ref[...], preferred_element_type=F32).astype(BF)
    keys, fresh_keys = both_keys[:KROWS], both_keys[KROWS:]
    values, fresh_values = both_values[:KROWS], both_values[KROWS:]

    row_band = (_iota((2 * QROWS, KROWS), 0) % QROWS) // TOK
    col_band = _iota((2 * QROWS, KROWS), 1) // TOK
    bias = jnp.where((row_band == _seat()) & (col_band == _brick()), FAR, 0.0).astype(F32)

    lane = _iota((QROWS, LANES), 1) % SLOT
    own_lane = _iota((TOK, LANES), 1) % SLOT
    logs = jnp.zeros((QROWS, LANES), F32)
    own_logs = jnp.zeros((TOK, LANES), F32)
    for pair in range(HEADS // 2):
        cut = slice(pair * LANES, (pair + 1) * LANES)
        mixed, low, high = _attend(queries_ref[:, cut], keys[:, cut], values[:, cut], bias)
        part_ref[:, :, cut] = mixed.astype(BF).reshape(NQ, TOK, LANES)
        logs = jnp.where(lane == 2 * pair, low, jnp.where(lane == 2 * pair + 1, high, logs))
        mixed, low, high = _attend(
            own_queries_ref[:, cut], fresh_keys[:, cut], fresh_values[:, cut], None
        )
        own_ref[:, cut] = mixed.astype(BF)
        own_logs = jnp.where(own_lane == 2 * pair, low, jnp.where(own_lane == 2 * pair + 1, high, own_logs))
    part_ref[:, :, C:] = _pack_logs(logs).reshape(NQ, TOK, LANES)
    own_ref[:, C:] = _pack_logs(own_logs)


def merge_kernel(part_ref, own_ref, projected_ref, hidden_ref, latent_ref, output_ref, level_ref, next_ref):
    next_ref[...] = hidden_ref[...]
    slot = _iota((LANES, C), 0)
    head = _iota((LANES, C), 1) // HEAD
    spread = jnp.where((slot % SLOT == head) & (slot < 3 * SLOT), 1.0, 0.0).astype(BF)
    logs = jnp.dot(part_ref[:, :, C:].reshape(QROWS, LANES), spread, preferred_element_type=F32)
    logs = logs.reshape(NQ, TOK, C)
    own_logs = jnp.dot(own_ref[:, C:], spread, preferred_element_type=F32)
    top = jnp.maximum(jnp.max(logs, axis=0), own_logs)
    weight = jnp.exp2(own_logs - top)
    total = weight
    mixed = weight * own_ref[:, :C].astype(F32)
    for index in range(NQ):
        weight = jnp.exp2(logs[index] - top)
        total = total + weight
        mixed = mixed + weight * part_ref[index, :, :C].astype(F32)
    attended = (mixed / total).astype(BF)
    out = jnp.dot(attended, output_ref[...], preferred_element_type=F32)
    level = latent_ref[...].reshape(TOK, C).astype(F32) + projected_ref[...] + out
    level_ref[...] = level.astype(BF).reshape(1, TOK, C)


def _call(kernel, out_shape, n_in, scratch=(), limit=16 * 2**20):
    specs = [pl.BlockSpec(memory_space=pltpu.VMEM)] * n_in
    several = isinstance(out_shape, tuple)
    whole = pl.BlockSpec(memory_space=pltpu.VMEM)
    return pl.pallas_call(
        kernel,
        out_shape=out_shape,
        in_specs=specs,
        out_specs=(whole,) * len(out_shape) if several else whole,
        scratch_shapes=list(scratch),
        compiler_params=pltpu.CompilerParams(vmem_limit_bytes=limit),
    )


def _share(block, groups):
    copies = jnp.broadcast_to(block[None], (len(groups[0]),) + block.shape)
    return lax.all_to_all(copies, "patch", 0, 0, axis_index_groups=groups)


def on_device(latent, stale_hidden, input_proj, query_proj, key_proj, value_proj, output_proj):
    shape = jax.ShapeDtypeStruct
    latents = _share(latent.reshape(TOK, C), BRICKS)
    blocks = _call(pack_kernel, shape((NK, STATS + 16, LANES), BF), 2)(latents, stale_hidden)
    blocks = lax.all_to_all(blocks, "patch", 0, 0, axis_index_groups=SEATS)
    queries, own_queries, projected, hidden = _call(
        query_kernel,
        (shape((QROWS, C), BF), shape((TOK, C), BF), shape((TOK, C), F32), shape((TOK, C), BF)),
        4,
        scratch=(pltpu.VMEM((QROWS, C), F32), pltpu.VMEM((QROWS, C), BF)),
    )(latents, blocks, input_proj, query_proj)
    parts, own = _call(attend_kernel, (shape((NQ, TOK, WIDE), BF), shape((TOK, WIDE), BF)), 6)(
        queries, own_queries, hidden, blocks, key_proj, value_proj
    )
    parts = lax.all_to_all(parts, "patch", 0, 0, axis_index_groups=BRICKS)
    return _call(merge_kernel, (shape((1, TOK, C), BF), shape((TOK, C), BF)), 6)(
        parts, own, projected, hidden, latent, output_proj
    )


def solution(mesh):
    rows = P(("batch", "patch"), None)
    return jax.shard_map(
        on_device,
        mesh=mesh,
        in_specs=(P(("batch", "patch"), None, None), rows, P(), P(), P(), P(), P()),
        out_specs=(P(("batch", "patch"), None, None), rows),
        check_vma=False,
    )
```

```python
import math

import jax
import jax.numpy as jnp
from jax import lax
from jax.experimental import pallas as pl
from jax.experimental.pallas import tpu as pltpu
from jax.sharding import PartitionSpec as P

C = 640
HEADS = 10
HEAD = 64
GROUP = 20
TOK = 32
BANDS = 128
LANES = 128
SLOT = 32
WIDE = C + LANES
STRIPS = TOK * C // LANES
STEP = math.log2(math.e) / math.sqrt(HEAD)
FAR = -1e30

PLACES = [(y, x, z) for y in range(8) for x in range(4) for z in range(4)]


def _groups(key):
    members = {}
    for index, place in enumerate(PLACES):
        members.setdefault(key(*place), []).append(index)
    return [members[k] for k in sorted(members)]


BRICKS = _groups(lambda y, x, z: (y // 2, z // 2))
SEATS = _groups(lambda y, x, z: (y % 2, x, z % 2))
NQ = len(BRICKS[0])
NK = len(SEATS[0])
QROWS = NQ * TOK
KROWS = NK * TOK
BF = jnp.bfloat16
F32 = jnp.float32


def _iota(shape, axis):
    return lax.broadcasted_iota(jnp.int32, shape, axis)


def _pieces(value):
    first = value.astype(BF).astype(F32)
    rest = value - first
    second = rest.astype(BF).astype(F32)
    return first, second, rest - second


def _same_group(shape, channel_axis):
    group_axis = 1 - channel_axis
    return jnp.where((_iota(shape, channel_axis) * 52429) >> 20 == _iota(shape, group_axis), 1.0, 0.0).astype(BF)


def _stack_pieces(*rows):
    which = _iota((16, rows[0].shape[1]), 0)
    stacked = jnp.zeros((16, rows[0].shape[1]), F32)
    for index, piece in enumerate(p for row in rows for p in _pieces(row)):
        stacked = jnp.where(which == index, piece, stacked)
    return stacked.astype(BF)


def _group_stats(cells):
    to_group = _same_group((C, LANES), 0)
    to_channel = _same_group((LANES, C), 1)

    def group_sums(row):
        sums = jnp.dot(_stack_pieces(row), to_group, preferred_element_type=F32)
        return jnp.sum(sums, axis=0, keepdims=True)

    center = group_sums(jnp.sum(cells, axis=0, keepdims=True)) * (1.0 / (cells.shape[0] * GROUP))
    centers = jnp.dot(_stack_pieces(center), to_channel, preferred_element_type=F32)
    shifted = cells - jnp.sum(centers, axis=0, keepdims=True)
    return center, group_sums(jnp.sum(jnp.square(shifted), axis=0, keepdims=True))


def _join_stats(blocks_ref, count):
    blocks = blocks_ref.shape[0]
    stats = blocks_ref[:, STRIPS:, :].reshape(blocks * 16, LANES)
    target = _iota((2 * blocks, blocks * 16), 0)
    source = _iota((2 * blocks, blocks * 16), 1) - (target % blocks) * 16 - (target // blocks) * 3
    picked = jnp.where((source >= 0) & (source < 3), 1.0, 0.0).astype(BF)
    stats = jnp.dot(picked, stats, preferred_element_type=F32)
    means, aways = stats[:blocks], stats[blocks:]
    mean = jnp.sum(means, axis=0, keepdims=True) * (1.0 / blocks)
    away = jnp.sum(aways + float(count) * jnp.square(means - mean), axis=0, keepdims=True)
    return mean, away


def _fill_blocks(out_ref, rows, stats):
    for index in range(out_ref.shape[0]):
        for part in range(C // LANES):
            out_ref[index, part * TOK : (part + 1) * TOK, :] = rows[:, part * LANES : (part + 1) * LANES]
        out_ref[index, STRIPS:, :] = stats


def _strips(blocks_ref, first, last):
    parts = [
        blocks_ref[first:last, part * TOK : (part + 1) * TOK, :].reshape((last - first) * TOK, LANES)
        for part in range(C // LANES)
    ]
    return jnp.concatenate(parts, axis=1)


def far_kernel(latent_ref, stale_ref, out_ref):
    center, away = _group_stats(latent_ref[...].reshape(TOK, C).astype(F32))
    _fill_blocks(out_ref, stale_ref[...], _stack_pieces(center, away))


def near_kernel(latent_ref, block_ref, out_ref):
    mean, away = _join_stats(block_ref, TOK * GROUP)
    _fill_blocks(out_ref, latent_ref[...].reshape(TOK, C), _stack_pieces(mean, away))


def _attend(q_pair, k_pair, v_pair, bias):
    rows = q_pair.shape[0]
    left = _iota((rows, LANES), 1) < HEAD
    zero = jnp.zeros_like(q_pair)
    both = jnp.concatenate([jnp.where(left, q_pair, zero), jnp.where(left, zero, q_pair)], axis=0)
    scores = lax.dot_general(both, k_pair, (((1,), (1,)), ((), ())), preferred_element_type=F32)
    if bias is not None:
        scores = scores + bias
    top = jnp.max(scores, axis=1, keepdims=True)
    weights = jnp.exp2((scores - top) * STEP).astype(BF)
    ones = jnp.ones_like(v_pair)
    sums = jnp.dot(weights, jnp.concatenate([v_pair, ones], axis=1), preferred_element_type=F32)
    total = sums[:, LANES:]
    mixed = sums[:, :LANES] / total
    logs = top * STEP + jnp.log2(total)
    return jnp.where(left, mixed[:rows], mixed[rows:]), logs[:rows], logs[rows:]


def _pack_logs(logs):
    first, second, third = _pieces(logs)
    lane = _iota(logs.shape, 1)
    return jnp.where(lane < SLOT, first, jnp.where(lane < 2 * SLOT, second, third)).astype(BF)


def _seat():
    me = lax.axis_index("patch")
    return ((me >> 4) & 1) * 8 + ((me >> 2) & 3) * 2 + (me & 1)


def _brick():
    me = lax.axis_index("patch")
    return (me >> 5) * 2 + ((me >> 1) & 1)


def query_kernel(
    latent_ref, input_ref, query_ref, queries_ref, own_queries_ref, projected_ref, hidden_ref, projected_all, hidden_all
):
    mine = pl.multiple_of(_seat() * TOK, TOK)

    mean, away = _join_stats(latent_ref, KROWS * GROUP)
    gain = lax.rsqrt(away * (1.0 / (KROWS * GROUP * NQ)) + 1e-06)
    spread = jnp.dot(_stack_pieces(mean, gain), _same_group((LANES, C), 1), preferred_element_type=F32)
    which = _iota((16, C), 0)
    center = jnp.sum(jnp.where(which < 3, spread, 0.0), axis=0, keepdims=True)
    gain = jnp.sum(jnp.where(which < 3, 0.0, spread), axis=0, keepdims=True)

    half = NQ // 2
    projections = []
    for index in range(2):
        cells = _strips(latent_ref, index * half, (index + 1) * half).astype(F32)
        normed = ((cells - center) * gain).astype(BF)
        projections.append(jnp.dot(normed, input_ref[...], preferred_element_type=F32))
    for index, projected in enumerate(projections):
        rows = slice(index * half * TOK, (index + 1) * half * TOK)
        projected_all[rows, :] = projected
        row_mean = jnp.mean(projected, axis=1, keepdims=True)
        shifted = projected - row_mean
        row_spread = jnp.mean(jnp.square(shifted), axis=1, keepdims=True)
        hidden = (shifted * lax.rsqrt(row_spread + 1e-05)).astype(BF)
        hidden_all[rows, :] = hidden
        queries_ref[rows, :] = jnp.dot(hidden, query_ref[...], preferred_element_type=F32).astype(BF)
    projected_ref[...] = projected_all[pl.ds(mine, TOK), :]
    hidden_ref[...] = hidden_all[pl.ds(mine, TOK), :]
    own_queries_ref[...] = queries_ref[pl.ds(mine, TOK), :]


def attend_kernel(queries_ref, own_queries_ref, hidden_ref, block_ref, key_ref, value_ref, part_ref, own_ref):
    both_hidden = jnp.concatenate([_strips(block_ref, 0, NK), hidden_ref[...]], axis=0)
    both_keys = jnp.dot(both_hidden, key_ref[...], preferred_element_type=F32).astype(BF)
    both_values = jnp.dot(both_hidden, value_ref[...], preferred_element_type=F32).astype(BF)
    keys, fresh_keys = both_keys[:KROWS], both_keys[KROWS:]
    values, fresh_values = both_values[:KROWS], both_values[KROWS:]

    row_band = (_iota((2 * QROWS, KROWS), 0) % QROWS) // TOK
    col_band = _iota((2 * QROWS, KROWS), 1) // TOK
    bias = jnp.where((row_band == _seat()) & (col_band == _brick()), FAR, 0.0).astype(F32)

    lane = _iota((QROWS, LANES), 1) % SLOT
    own_lane = _iota((TOK, LANES), 1) % SLOT
    logs = jnp.zeros((QROWS, LANES), F32)
    own_logs = jnp.zeros((TOK, LANES), F32)
    for pair in range(HEADS // 2):
        cut = slice(pair * LANES, (pair + 1) * LANES)
        mixed, low, high = _attend(queries_ref[:, cut], keys[:, cut], values[:, cut], bias)
        part_ref[:, :, cut] = mixed.astype(BF).reshape(NQ, TOK, LANES)
        logs = jnp.where(lane == 2 * pair, low, jnp.where(lane == 2 * pair + 1, high, logs))
        mixed, low, high = _attend(
            own_queries_ref[:, cut], fresh_keys[:, cut], fresh_values[:, cut], None
        )
        own_ref[:, cut] = mixed.astype(BF)
        own_logs = jnp.where(own_lane == 2 * pair, low, jnp.where(own_lane == 2 * pair + 1, high, own_logs))
    part_ref[:, :, C:] = _pack_logs(logs).reshape(NQ, TOK, LANES)
    own_ref[:, C:] = _pack_logs(own_logs)


def merge_kernel(part_ref, own_ref, projected_ref, hidden_ref, latent_ref, output_ref, level_ref, next_ref):
    next_ref[...] = hidden_ref[...]
    slot = _iota((LANES, C), 0)
    head = _iota((LANES, C), 1) // HEAD
    spread = jnp.where((slot % SLOT == head) & (slot < 3 * SLOT), 1.0, 0.0).astype(BF)
    logs = jnp.dot(part_ref[:, :, C:].reshape(QROWS, LANES), spread, preferred_element_type=F32)
    logs = logs.reshape(NQ, TOK, C)
    own_logs = jnp.dot(own_ref[:, C:], spread, preferred_element_type=F32)
    top = jnp.maximum(jnp.max(logs, axis=0), own_logs)
    weight = jnp.exp2(own_logs - top)
    total = weight
    mixed = weight * own_ref[:, :C].astype(F32)
    for index in range(NQ):
        weight = jnp.exp2(logs[index] - top)
        total = total + weight
        mixed = mixed + weight * part_ref[index, :, :C].astype(F32)
    attended = (mixed / total).astype(BF)
    out = jnp.dot(attended, output_ref[...], preferred_element_type=F32)
    level = latent_ref[...].reshape(TOK, C).astype(F32) + projected_ref[...] + out
    level_ref[...] = level.astype(BF).reshape(1, TOK, C)


def _call(kernel, out_shape, n_in, scratch=(), limit=16 * 2**20):
    specs = [pl.BlockSpec(memory_space=pltpu.VMEM)] * n_in
    several = isinstance(out_shape, tuple)
    whole = pl.BlockSpec(memory_space=pltpu.VMEM)
    return pl.pallas_call(
        kernel,
        out_shape=out_shape,
        in_specs=specs,
        out_specs=(whole,) * len(out_shape) if several else whole,
        scratch_shapes=list(scratch),
        compiler_params=pltpu.CompilerParams(vmem_limit_bytes=limit),
    )


def on_device(latent, stale_hidden, input_proj, query_proj, key_proj, value_proj, output_proj):
    shape = jax.ShapeDtypeStruct
    stale = _call(far_kernel, shape((NK, STRIPS + 16, LANES), BF), 2)(latent, stale_hidden)
    stale = lax.all_to_all(stale, "patch", 0, 0, axis_index_groups=SEATS)
    latents = _call(near_kernel, shape((NQ, STRIPS + 16, LANES), BF), 2)(latent, stale)
    latents = lax.all_to_all(latents, "patch", 0, 0, axis_index_groups=BRICKS)
    queries, own_queries, projected, hidden = _call(
        query_kernel,
        (shape((QROWS, C), BF), shape((TOK, C), BF), shape((TOK, C), F32), shape((TOK, C), BF)),
        3,
        scratch=(pltpu.VMEM((QROWS, C), F32), pltpu.VMEM((QROWS, C), BF)),
    )(latents, input_proj, query_proj)
    parts, own = _call(attend_kernel, (shape((NQ, TOK, WIDE), BF), shape((TOK, WIDE), BF)), 6)(
        queries, own_queries, hidden, stale, key_proj, value_proj
    )
    parts = lax.all_to_all(parts, "patch", 0, 0, axis_index_groups=BRICKS)
    return _call(merge_kernel, (shape((1, TOK, C), BF), shape((TOK, C), BF)), 6)(
        parts, own, projected, hidden, latent, output_proj
    )


def solution(mesh):
    rows = P(("batch", "patch"), None)
    return jax.shard_map(
        on_device,
        mesh=mesh,
        in_specs=(P(("batch", "patch"), None, None), rows, P(), P(), P(), P(), P()),
        out_specs=(P(("batch", "patch"), None, None), rows),
        check_vma=False,
    )
```

```python
import math

import jax
import jax.numpy as jnp
from jax import lax
from jax.experimental import pallas as pl
from jax.experimental.pallas import tpu as pltpu
from jax.sharding import PartitionSpec as P

C = 640
HEADS = 10
HEAD = 64
GROUP = 20
TOK = 32
BANDS = 128
LANES = 128
SLOT = 32
WIDE = C + LANES
STRIPS = TOK * C // LANES
STEP = math.log2(math.e) / math.sqrt(HEAD)
FAR = -1e30

PLACES = [(y, x, z) for y in range(8) for x in range(4) for z in range(4)]


def _groups(key):
    members = {}
    for index, place in enumerate(PLACES):
        members.setdefault(key(*place), []).append(index)
    return [members[k] for k in sorted(members)]


BRICKS = _groups(lambda y, x, z: (y // 2, z // 2))
SEATS = _groups(lambda y, x, z: (y % 2, x, z % 2))
NQ = len(BRICKS[0])
NK = len(SEATS[0])
QROWS = NQ * TOK
KROWS = NK * TOK
BF = jnp.bfloat16
F32 = jnp.float32


def _iota(shape, axis):
    return lax.broadcasted_iota(jnp.int32, shape, axis)


def _pieces(value):
    first = value.astype(BF).astype(F32)
    rest = value - first
    second = rest.astype(BF).astype(F32)
    return first, second, rest - second


def _same_group(shape, channel_axis):
    group_axis = 1 - channel_axis
    return jnp.where((_iota(shape, channel_axis) * 52429) >> 20 == _iota(shape, group_axis), 1.0, 0.0).astype(BF)


def _stack_pieces(*rows):
    which = _iota((16, rows[0].shape[1]), 0)
    stacked = jnp.zeros((16, rows[0].shape[1]), F32)
    for index, piece in enumerate(p for row in rows for p in _pieces(row)):
        stacked = jnp.where(which == index, piece, stacked)
    return stacked.astype(BF)


def _group_stats(cells):
    to_group = _same_group((C, LANES), 0)
    to_channel = _same_group((LANES, C), 1)

    def group_sums(row):
        sums = jnp.dot(_stack_pieces(row), to_group, preferred_element_type=F32)
        return jnp.sum(sums, axis=0, keepdims=True)

    center = group_sums(jnp.sum(cells, axis=0, keepdims=True)) * (1.0 / (cells.shape[0] * GROUP))
    centers = jnp.dot(_stack_pieces(center), to_channel, preferred_element_type=F32)
    shifted = cells - jnp.sum(centers, axis=0, keepdims=True)
    return center, group_sums(jnp.sum(jnp.square(shifted), axis=0, keepdims=True))


def _join_stats(blocks_ref, count):
    blocks = blocks_ref.shape[0]
    stats = blocks_ref[:, STRIPS:, :].reshape(blocks * 16, LANES)
    target = _iota((2 * blocks, blocks * 16), 0)
    source = _iota((2 * blocks, blocks * 16), 1) - (target % blocks) * 16 - (target // blocks) * 3
    picked = jnp.where((source >= 0) & (source < 3), 1.0, 0.0).astype(BF)
    stats = jnp.dot(picked, stats, preferred_element_type=F32)
    means, aways = stats[:blocks], stats[blocks:]
    mean = jnp.sum(means, axis=0, keepdims=True) * (1.0 / blocks)
    away = jnp.sum(aways + float(count) * jnp.square(means - mean), axis=0, keepdims=True)
    return mean, away


def _fill_blocks(out_ref, rows, stats):
    for index in range(out_ref.shape[0]):
        for part in range(C // LANES):
            out_ref[index, part * TOK : (part + 1) * TOK, :] = rows[:, part * LANES : (part + 1) * LANES]
        out_ref[index, STRIPS:, :] = stats


def _strips(blocks_ref, first, last):
    parts = [
        blocks_ref[first:last, part * TOK : (part + 1) * TOK, :].reshape((last - first) * TOK, LANES)
        for part in range(C // LANES)
    ]
    return jnp.concatenate(parts, axis=1)


def far_kernel(latent_ref, stale_ref, out_ref, latent, stale, arrived):
    pulls = (
        pltpu.make_async_copy(latent_ref, latent, arrived.at[0]),
        pltpu.make_async_copy(stale_ref, stale, arrived.at[1]),
    )
    for pull in pulls:
        pull.start()
    for pull in pulls:
        pull.wait()
    center, away = _group_stats(latent[...].reshape(TOK, C).astype(F32))
    _fill_blocks(out_ref, stale[...], _stack_pieces(center, away))


def near_kernel(latent_ref, block_ref, out_ref):
    mean, away = _join_stats(block_ref, TOK * GROUP)
    _fill_blocks(out_ref, latent_ref[...].reshape(TOK, C), _stack_pieces(mean, away))


def _attend(q_pair, k_pair, v_pair, bias):
    rows = q_pair.shape[0]
    left = _iota((rows, LANES), 1) < HEAD
    zero = jnp.zeros_like(q_pair)
    both = jnp.concatenate([jnp.where(left, q_pair, zero), jnp.where(left, zero, q_pair)], axis=0)
    scores = lax.dot_general(both, k_pair, (((1,), (1,)), ((), ())), preferred_element_type=F32)
    if bias is not None:
        scores = scores + bias
    top = jnp.max(scores, axis=1, keepdims=True)
    weights = jnp.exp2((scores - top) * STEP).astype(BF)
    ones = jnp.ones_like(v_pair)
    sums = jnp.dot(weights, jnp.concatenate([v_pair, ones], axis=1), preferred_element_type=F32)
    total = sums[:, LANES:]
    mixed = sums[:, :LANES] / total
    logs = top * STEP + jnp.log2(total)
    return jnp.where(left, mixed[:rows], mixed[rows:]), logs[:rows], logs[rows:]


def _pack_logs(logs):
    first, second, third = _pieces(logs)
    lane = _iota(logs.shape, 1)
    return jnp.where(lane < SLOT, first, jnp.where(lane < 2 * SLOT, second, third)).astype(BF)


def _seat():
    me = lax.axis_index("patch")
    return ((me >> 4) & 1) * 8 + ((me >> 2) & 3) * 2 + (me & 1)


def _brick():
    me = lax.axis_index("patch")
    return (me >> 5) * 2 + ((me >> 1) & 1)


def query_kernel(
    latent_ref, input_ref, query_ref, queries_ref, own_queries_ref, projected_ref, hidden_ref, projected_all, hidden_all
):
    mine = pl.multiple_of(_seat() * TOK, TOK)

    mean, away = _join_stats(latent_ref, KROWS * GROUP)
    gain = lax.rsqrt(away * (1.0 / (KROWS * GROUP * NQ)) + 1e-06)
    spread = jnp.dot(_stack_pieces(mean, gain), _same_group((LANES, C), 1), preferred_element_type=F32)
    which = _iota((16, C), 0)
    center = jnp.sum(jnp.where(which < 3, spread, 0.0), axis=0, keepdims=True)
    gain = jnp.sum(jnp.where(which < 3, 0.0, spread), axis=0, keepdims=True)

    half = NQ // 2
    projections = []
    for index in range(2):
        cells = _strips(latent_ref, index * half, (index + 1) * half).astype(F32)
        normed = ((cells - center) * gain).astype(BF)
        projections.append(jnp.dot(normed, input_ref[...], preferred_element_type=F32))
    for index, projected in enumerate(projections):
        rows = slice(index * half * TOK, (index + 1) * half * TOK)
        projected_all[rows, :] = projected
        row_mean = jnp.mean(projected, axis=1, keepdims=True)
        shifted = projected - row_mean
        row_spread = jnp.mean(jnp.square(shifted), axis=1, keepdims=True)
        hidden = (shifted * lax.rsqrt(row_spread + 1e-05)).astype(BF)
        hidden_all[rows, :] = hidden
        queries_ref[rows, :] = jnp.dot(hidden, query_ref[...], preferred_element_type=F32).astype(BF)
    projected_ref[...] = projected_all[pl.ds(mine, TOK), :]
    hidden_ref[...] = hidden_all[pl.ds(mine, TOK), :]
    own_queries_ref[...] = queries_ref[pl.ds(mine, TOK), :]


def attend_kernel(queries_ref, own_queries_ref, hidden_ref, block_ref, key_ref, value_ref, part_ref, own_ref):
    both_hidden = jnp.concatenate([_strips(block_ref, 0, NK), hidden_ref[...]], axis=0)
    both_keys = jnp.dot(both_hidden, key_ref[...], preferred_element_type=F32).astype(BF)
    both_values = jnp.dot(both_hidden, value_ref[...], preferred_element_type=F32).astype(BF)
    keys, fresh_keys = both_keys[:KROWS], both_keys[KROWS:]
    values, fresh_values = both_values[:KROWS], both_values[KROWS:]

    row_band = (_iota((2 * QROWS, KROWS), 0) % QROWS) // TOK
    col_band = _iota((2 * QROWS, KROWS), 1) // TOK
    bias = jnp.where((row_band == _seat()) & (col_band == _brick()), FAR, 0.0).astype(F32)

    lane = _iota((QROWS, LANES), 1) % SLOT
    own_lane = _iota((TOK, LANES), 1) % SLOT
    logs = jnp.zeros((QROWS, LANES), F32)
    own_logs = jnp.zeros((TOK, LANES), F32)
    for pair in range(HEADS // 2):
        cut = slice(pair * LANES, (pair + 1) * LANES)
        mixed, low, high = _attend(queries_ref[:, cut], keys[:, cut], values[:, cut], bias)
        part_ref[:, :, cut] = mixed.astype(BF).reshape(NQ, TOK, LANES)
        logs = jnp.where(lane == 2 * pair, low, jnp.where(lane == 2 * pair + 1, high, logs))
        mixed, low, high = _attend(
            own_queries_ref[:, cut], fresh_keys[:, cut], fresh_values[:, cut], None
        )
        own_ref[:, cut] = mixed.astype(BF)
        own_logs = jnp.where(own_lane == 2 * pair, low, jnp.where(own_lane == 2 * pair + 1, high, own_logs))
    part_ref[:, :, C:] = _pack_logs(logs).reshape(NQ, TOK, LANES)
    own_ref[:, C:] = _pack_logs(own_logs)


def merge_kernel(part_ref, own_ref, projected_ref, hidden_ref, latent_ref, output_ref, level_ref, next_ref):
    next_ref[...] = hidden_ref[...]
    slot = _iota((LANES, C), 0)
    head = _iota((LANES, C), 1) // HEAD
    spread = jnp.where((slot % SLOT == head) & (slot < 3 * SLOT), 1.0, 0.0).astype(BF)
    logs = jnp.dot(part_ref[:, :, C:].reshape(QROWS, LANES), spread, preferred_element_type=F32)
    logs = logs.reshape(NQ, TOK, C)
    own_logs = jnp.dot(own_ref[:, C:], spread, preferred_element_type=F32)
    top = jnp.maximum(jnp.max(logs, axis=0), own_logs)
    weight = jnp.exp2(own_logs - top)
    total = weight
    mixed = weight * own_ref[:, :C].astype(F32)
    for index in range(NQ):
        weight = jnp.exp2(logs[index] - top)
        total = total + weight
        mixed = mixed + weight * part_ref[index, :, :C].astype(F32)
    attended = (mixed / total).astype(BF)
    out = jnp.dot(attended, output_ref[...], preferred_element_type=F32)
    level = latent_ref[...].reshape(TOK, C).astype(F32) + projected_ref[...] + out
    level_ref[...] = level.astype(BF).reshape(1, TOK, C)


def _call(kernel, out_shape, n_in, place=pltpu.VMEM, scratch=(), limit=16 * 2**20):
    specs = [pl.BlockSpec(memory_space=place)] * n_in
    several = isinstance(out_shape, tuple)
    whole = pl.BlockSpec(memory_space=pltpu.VMEM)
    return pl.pallas_call(
        kernel,
        out_shape=out_shape,
        in_specs=specs,
        out_specs=(whole,) * len(out_shape) if several else whole,
        scratch_shapes=list(scratch),
        compiler_params=pltpu.CompilerParams(vmem_limit_bytes=limit),
    )


def on_device(latent, stale_hidden, input_proj, query_proj, key_proj, value_proj, output_proj):
    shape = jax.ShapeDtypeStruct
    stale = _call(
        far_kernel,
        shape((NK, STRIPS + 16, LANES), BF),
        2,
        place=pltpu.HBM,
        scratch=(pltpu.VMEM(latent.shape, BF), pltpu.VMEM(stale_hidden.shape, BF), pltpu.SemaphoreType.DMA((2,))),
    )(latent, stale_hidden)
    stale = lax.all_to_all(stale, "patch", 0, 0, axis_index_groups=SEATS)
    latents = _call(near_kernel, shape((NQ, STRIPS + 16, LANES), BF), 2)(latent, stale)
    latents = lax.all_to_all(latents, "patch", 0, 0, axis_index_groups=BRICKS)
    queries, own_queries, projected, hidden = _call(
        query_kernel,
        (shape((QROWS, C), BF), shape((TOK, C), BF), shape((TOK, C), F32), shape((TOK, C), BF)),
        3,
        scratch=(pltpu.VMEM((QROWS, C), F32), pltpu.VMEM((QROWS, C), BF)),
    )(latents, input_proj, query_proj)
    parts, own = _call(attend_kernel, (shape((NQ, TOK, WIDE), BF), shape((TOK, WIDE), BF)), 6)(
        queries, own_queries, hidden, stale, key_proj, value_proj
    )
    parts = lax.all_to_all(parts, "patch", 0, 0, axis_index_groups=BRICKS)
    return _call(merge_kernel, (shape((1, TOK, C), BF), shape((TOK, C), BF)), 6)(
        parts, own, projected, hidden, latent, output_proj
    )


def solution(mesh):
    rows = P(("batch", "patch"), None)
    return jax.shard_map(
        on_device,
        mesh=mesh,
        in_specs=(P(("batch", "patch"), None, None), rows, P(), P(), P(), P(), P()),
        out_specs=(P(("batch", "patch"), None, None), rows),
        check_vma=False,
    )
```

```python
import math

import jax
import jax.numpy as jnp
from jax import lax
from jax.experimental import pallas as pl
from jax.experimental.pallas import tpu as pltpu
from jax.sharding import PartitionSpec as P

C = 640
HEADS = 10
HEAD = 64
GROUP = 20
TOK = 32
BANDS = 128
LANES = 128
SLOT = 32
WIDE = C + LANES
STATS = TOK * C // LANES
STEP = math.log2(math.e) / math.sqrt(HEAD)
FAR = -1e30

PLACES = [(y, x, z) for y in range(8) for x in range(4) for z in range(4)]


def _groups(key):
    members = {}
    for index, place in enumerate(PLACES):
        members.setdefault(key(*place), []).append(index)
    return [members[k] for k in sorted(members)]


BRICKS = _groups(lambda y, x, z: (y, z // 2))
SEATS = _groups(lambda y, x, z: (x, z % 2))
NQ = len(BRICKS[0])
NK = len(SEATS[0])
QROWS = NQ * TOK
KROWS = NK * TOK
BF = jnp.bfloat16
F32 = jnp.float32


def _iota(shape, axis):
    return lax.broadcasted_iota(jnp.int32, shape, axis)


def _pieces(value):
    first = value.astype(BF).astype(F32)
    rest = value - first
    second = rest.astype(BF).astype(F32)
    return first, second, rest - second


def _same_group(shape, channel_axis):
    group_axis = 1 - channel_axis
    return jnp.where((_iota(shape, channel_axis) * 52429) >> 20 == _iota(shape, group_axis), 1.0, 0.0).astype(BF)


def _stack_pieces(*rows):
    which = _iota((16, rows[0].shape[1]), 0)
    stacked = jnp.zeros((16, rows[0].shape[1]), F32)
    for index, piece in enumerate(p for row in rows for p in _pieces(row)):
        stacked = jnp.where(which == index, piece, stacked)
    return stacked.astype(BF)


def pack_kernel(latent_ref, stale_ref, out_ref):
    cells = latent_ref[...].astype(F32).reshape(QROWS, C)
    to_group = _same_group((C, LANES), 0)
    to_channel = _same_group((LANES, C), 1)

    def group_sums(row):
        sums = jnp.dot(_stack_pieces(row), to_group, preferred_element_type=F32)
        return jnp.sum(sums, axis=0, keepdims=True)

    center = group_sums(jnp.sum(cells, axis=0, keepdims=True)) * (1.0 / (QROWS * GROUP))
    centers = jnp.dot(_stack_pieces(center), to_channel, preferred_element_type=F32)
    shifted = cells - jnp.sum(centers, axis=0, keepdims=True)
    away = group_sums(jnp.sum(jnp.square(shifted), axis=0, keepdims=True))
    stats = _stack_pieces(center, away)
    for index in range(NK):
        for part in range(C // LANES):
            out_ref[index, part * TOK : (part + 1) * TOK, :] = stale_ref[:, part * LANES : (part + 1) * LANES]
        out_ref[index, STATS:, :] = stats


def _attend_own(queries, keys, values, out_ref):
    head = _iota((TOK, C), 1) // HEAD
    zero = jnp.zeros_like(queries)
    stacked = jnp.concatenate([jnp.where(head == h, queries, zero) for h in range(HEADS)], axis=0)
    scores = lax.dot_general(stacked, keys, (((1,), (1,)), ((), ())), preferred_element_type=F32)
    top = jnp.max(scores, axis=1, keepdims=True)
    weights = jnp.exp2((scores - top) * STEP).astype(BF)
    ones = jnp.ones((TOK, LANES), BF)
    sums = jnp.dot(weights, jnp.concatenate([values, ones], axis=1), preferred_element_type=F32)
    total = sums[:, C:]
    scale = 1.0 / total
    logs = top * STEP + jnp.log2(total)
    left = _iota((TOK, LANES), 1) < HEAD
    lane = _iota((TOK, LANES), 1) % SLOT
    packed = jnp.zeros((TOK, LANES), F32)
    for pair in range(HEADS // 2):
        cut = slice(pair * LANES, (pair + 1) * LANES)
        low = slice(2 * pair * TOK, (2 * pair + 1) * TOK)
        high = slice((2 * pair + 1) * TOK, (2 * pair + 2) * TOK)
        out_ref[:, cut] = jnp.where(left, sums[low, cut] * scale[low], sums[high, cut] * scale[high]).astype(BF)
        packed = jnp.where(lane == 2 * pair, logs[low], jnp.where(lane == 2 * pair + 1, logs[high], packed))
    out_ref[:, C:] = _pack_logs(packed)


def _attend(q_pair, k_pair, v_pair, bias):
    rows = q_pair.shape[0]
    left = _iota((rows, LANES), 1) < HEAD
    zero = jnp.zeros_like(q_pair)
    both = jnp.concatenate([jnp.where(left, q_pair, zero), jnp.where(left, zero, q_pair)], axis=0)
    scores = lax.dot_general(both, k_pair, (((1,), (1,)), ((), ())), preferred_element_type=F32)
    if bias is not None:
        scores = scores + bias
    top = jnp.max(scores, axis=1, keepdims=True)
    weights = jnp.exp2((scores - top) * STEP).astype(BF)
    ones = jnp.ones_like(v_pair)
    sums = jnp.dot(weights, jnp.concatenate([v_pair, ones], axis=1), preferred_element_type=F32)
    total = sums[:, LANES:]
    mixed = sums[:, :LANES] / total
    logs = top * STEP + jnp.log2(total)
    return jnp.where(left, mixed[:rows], mixed[rows:]), logs[:rows], logs[rows:]


def _pack_logs(logs):
    first, second, third = _pieces(logs)
    lane = _iota(logs.shape, 1)
    return jnp.where(lane < SLOT, first, jnp.where(lane < 2 * SLOT, second, third)).astype(BF)


def _seat():
    me = lax.axis_index("patch")
    return ((me >> 2) & 3) * 2 + (me & 1)


def _brick():
    me = lax.axis_index("patch")
    return (me >> 4) * 2 + ((me >> 1) & 1)


def query_kernel(
    latent_ref, block_ref, input_ref, query_ref, queries_ref, own_queries_ref, projected_ref, hidden_ref, projected_all, hidden_all
):
    mine = pl.multiple_of(_seat() * TOK, TOK)

    stats = block_ref[:, STATS:, :].reshape(NK * 16, LANES)
    target = _iota((2 * NK, NK * 16), 0)
    source = _iota((2 * NK, NK * 16), 1) - (target % NK) * 16 - (target // NK) * 3
    picked = jnp.where((source >= 0) & (source < 3), 1.0, 0.0).astype(BF)
    stats = jnp.dot(picked, stats, preferred_element_type=F32)
    parts_mean, parts_away = stats[:NK], stats[NK:]
    mean = jnp.sum(parts_mean, axis=0, keepdims=True) * (1.0 / NK)
    cell_count = float(QROWS * GROUP)
    away = jnp.sum(parts_away + cell_count * jnp.square(parts_mean - mean), axis=0, keepdims=True)
    gain = lax.rsqrt(away * (1.0 / (cell_count * NK)) + 1e-06)
    spread = jnp.dot(_stack_pieces(mean, gain), _same_group((LANES, C), 1), preferred_element_type=F32)
    which = _iota((16, C), 0)
    center = jnp.sum(jnp.where(which < 3, spread, 0.0), axis=0, keepdims=True)
    gain = jnp.sum(jnp.where(which < 3, 0.0, spread), axis=0, keepdims=True)
    step = QROWS // 2
    starts = range(0, QROWS, step)
    projections = []
    for start in starts:
        cells = latent_ref[start // TOK : (start + step) // TOK].astype(F32).reshape(step, C)
        normed = ((cells - center) * gain).astype(BF)
        projections.append(jnp.dot(normed, input_ref[...], preferred_element_type=F32))
    for start, projected in zip(starts, projections):
        rows = slice(start, start + step)
        projected_all[rows, :] = projected
        row_mean = jnp.mean(projected, axis=1, keepdims=True)
        shifted = projected - row_mean
        row_spread = jnp.mean(jnp.square(shifted), axis=1, keepdims=True)
        hidden = (shifted * lax.rsqrt(row_spread + 1e-05)).astype(BF)
        hidden_all[rows, :] = hidden
        queries_ref[rows, :] = jnp.dot(hidden, query_ref[...], preferred_element_type=F32).astype(BF)
    projected_ref[...] = projected_all[pl.ds(mine, TOK), :]
    hidden_ref[...] = hidden_all[pl.ds(mine, TOK), :]
    own_queries_ref[...] = queries_ref[pl.ds(mine, TOK), :]


def attend_kernel(queries_ref, own_queries_ref, hidden_ref, block_ref, key_ref, value_ref, part_ref, own_ref):
    strips = [block_ref[:, part * TOK : (part + 1) * TOK, :].reshape(KROWS, LANES) for part in range(C // LANES)]
    both_hidden = jnp.concatenate([jnp.concatenate(strips, axis=1), hidden_ref[...]], axis=0)
    both_keys = jnp.dot(both_hidden, key_ref[...], preferred_element_type=F32).astype(BF)
    both_values = jnp.dot(both_hidden, value_ref[...], preferred_element_type=F32).astype(BF)
    keys, fresh_keys = both_keys[:KROWS], both_keys[KROWS:]
    values, fresh_values = both_values[:KROWS], both_values[KROWS:]

    row_band = (_iota((2 * QROWS, KROWS), 0) % QROWS) // TOK
    col_band = _iota((2 * QROWS, KROWS), 1) // TOK
    bias = jnp.where((row_band == _seat()) & (col_band == _brick()), FAR, 0.0).astype(F32)

    lane = _iota((QROWS, LANES), 1) % SLOT
    logs = jnp.zeros((QROWS, LANES), F32)
    for pair in range(HEADS // 2):
        cut = slice(pair * LANES, (pair + 1) * LANES)
        mixed, low, high = _attend(queries_ref[:, cut], keys[:, cut], values[:, cut], bias)
        part_ref[:, :, cut] = mixed.astype(BF).reshape(NQ, TOK, LANES)
        logs = jnp.where(lane == 2 * pair, low, jnp.where(lane == 2 * pair + 1, high, logs))
    part_ref[:, :, C:] = _pack_logs(logs).reshape(NQ, TOK, LANES)
    _attend_own(own_queries_ref[...], fresh_keys, fresh_values, own_ref)


def merge_kernel(part_ref, own_ref, projected_ref, hidden_ref, latent_ref, output_ref, level_ref, next_ref):
    next_ref[...] = hidden_ref[...]
    slot = _iota((LANES, C), 0)
    head = _iota((LANES, C), 1) // HEAD
    spread = jnp.where((slot % SLOT == head) & (slot < 3 * SLOT), 1.0, 0.0).astype(BF)
    logs = jnp.dot(part_ref[:, :, C:].reshape(QROWS, LANES), spread, preferred_element_type=F32)
    logs = logs.reshape(NQ, TOK, C)
    own_logs = jnp.dot(own_ref[:, C:], spread, preferred_element_type=F32)
    top = jnp.maximum(jnp.max(logs, axis=0), own_logs)
    weight = jnp.exp2(own_logs - top)
    total = weight
    mixed = weight * own_ref[:, :C].astype(F32)
    for index in range(NQ):
        weight = jnp.exp2(logs[index] - top)
        total = total + weight
        mixed = mixed + weight * part_ref[index, :, :C].astype(F32)
    attended = (mixed / total).astype(BF)
    out = jnp.dot(attended, output_ref[...], preferred_element_type=F32)
    level = latent_ref[...].reshape(TOK, C).astype(F32) + projected_ref[...] + out
    level_ref[...] = level.astype(BF).reshape(1, TOK, C)


def _call(kernel, out_shape, n_in, scratch=(), limit=16 * 2**20):
    specs = [pl.BlockSpec(memory_space=pltpu.VMEM)] * n_in
    several = isinstance(out_shape, tuple)
    whole = pl.BlockSpec(memory_space=pltpu.VMEM)
    return pl.pallas_call(
        kernel,
        out_shape=out_shape,
        in_specs=specs,
        out_specs=(whole,) * len(out_shape) if several else whole,
        scratch_shapes=list(scratch),
        compiler_params=pltpu.CompilerParams(vmem_limit_bytes=limit),
    )


def _share(block, groups):
    copies = jnp.broadcast_to(block[None], (len(groups[0]),) + block.shape)
    return lax.all_to_all(copies, "patch", 0, 0, axis_index_groups=groups)


def on_device(latent, stale_hidden, input_proj, query_proj, key_proj, value_proj, output_proj):
    shape = jax.ShapeDtypeStruct
    latents = _share(latent.reshape(TOK, C), BRICKS)
    blocks = _call(pack_kernel, shape((NK, STATS + 16, LANES), BF), 2)(latents, stale_hidden)
    blocks = lax.all_to_all(blocks, "patch", 0, 0, axis_index_groups=SEATS)
    queries, own_queries, projected, hidden = _call(
        query_kernel,
        (shape((QROWS, C), BF), shape((TOK, C), BF), shape((TOK, C), F32), shape((TOK, C), BF)),
        4,
        scratch=(pltpu.VMEM((QROWS, C), F32), pltpu.VMEM((QROWS, C), BF)),
    )(latents, blocks, input_proj, query_proj)
    parts, own = _call(attend_kernel, (shape((NQ, TOK, WIDE), BF), shape((TOK, WIDE), BF)), 6)(
        queries, own_queries, hidden, blocks, key_proj, value_proj
    )
    parts = lax.all_to_all(parts, "patch", 0, 0, axis_index_groups=BRICKS)
    return _call(merge_kernel, (shape((1, TOK, C), BF), shape((TOK, C), BF)), 6)(
        parts, own, projected, hidden, latent, output_proj
    )


def solution(mesh):
    rows = P(("batch", "patch"), None)
    return jax.shard_map(
        on_device,
        mesh=mesh,
        in_specs=(P(("batch", "patch"), None, None), rows, P(), P(), P(), P(), P()),
        out_specs=(P(("batch", "patch"), None, None), rows),
        check_vma=False,
    )
```

```python
import math

import jax
import jax.numpy as jnp
from jax import lax
from jax.experimental import pallas as pl
from jax.experimental.pallas import tpu as pltpu
from jax.sharding import PartitionSpec as P

C = 640
HEADS = 10
HEAD = 64
GROUP = 20
TOK = 32
BANDS = 128
LANES = 128
SLOT = 32
WIDE = C + LANES
STATS = TOK * C // LANES
STAT_ROWS = 8
STEP = math.log2(math.e) / math.sqrt(HEAD)
FAR = -1e30

PLACES = [(y, x, z) for y in range(8) for x in range(4) for z in range(4)]


def _groups(key):
    members = {}
    for index, place in enumerate(PLACES):
        members.setdefault(key(*place), []).append(index)
    return [members[k] for k in sorted(members)]


BRICKS = _groups(lambda y, x, z: (y, z // 2))
SEATS = _groups(lambda y, x, z: (x, z % 2))
NQ = len(BRICKS[0])
NK = len(SEATS[0])
QROWS = NQ * TOK
KROWS = NK * TOK
BF = jnp.bfloat16
F32 = jnp.float32


def _iota(shape, axis):
    return lax.broadcasted_iota(jnp.int32, shape, axis)


def _pieces(value):
    first = value.astype(BF).astype(F32)
    rest = value - first
    second = rest.astype(BF).astype(F32)
    return first, second, rest - second


def _same_group(shape, channel_axis):
    group_axis = 1 - channel_axis
    return jnp.where((_iota(shape, channel_axis) * 52429) >> 20 == _iota(shape, group_axis), 1.0, 0.0).astype(BF)


def _stack_pieces(*rows, height=16):
    which = _iota((height, rows[0].shape[1]), 0)
    stacked = jnp.zeros((height, rows[0].shape[1]), F32)
    for index, piece in enumerate(p for row in rows for p in _pieces(row)):
        stacked = jnp.where(which == index, piece, stacked)
    return stacked.astype(BF)


def pack_kernel(latent_ref, stale_ref, out_ref):
    cells = latent_ref[...].astype(F32).reshape(QROWS, C)
    to_group = _same_group((C, LANES), 0)
    to_channel = _same_group((LANES, C), 1)

    def group_sums(row):
        sums = jnp.dot(_stack_pieces(row), to_group, preferred_element_type=F32)
        return jnp.sum(sums, axis=0, keepdims=True)

    center = group_sums(jnp.sum(cells, axis=0, keepdims=True)) * (1.0 / (QROWS * GROUP))
    centers = jnp.dot(_stack_pieces(center), to_channel, preferred_element_type=F32)
    shifted = cells - jnp.sum(centers, axis=0, keepdims=True)
    away = group_sums(jnp.sum(jnp.square(shifted), axis=0, keepdims=True))
    stats = _stack_pieces(center, away, height=STAT_ROWS)
    for index in range(NK):
        for part in range(C // LANES):
            out_ref[index, part * TOK : (part + 1) * TOK, :] = stale_ref[:, part * LANES : (part + 1) * LANES]
        out_ref[index, STATS:, :] = stats


def _attend_own(queries, keys, values, out_ref):
    head = _iota((TOK, C), 1) // HEAD
    zero = jnp.zeros_like(queries)
    stacked = jnp.concatenate([jnp.where(head == h, queries, zero) for h in range(HEADS)], axis=0)
    scores = lax.dot_general(stacked, keys, (((1,), (1,)), ((), ())), preferred_element_type=F32)
    top = jnp.max(scores, axis=1, keepdims=True)
    weights = jnp.exp2((scores - top) * STEP).astype(BF)
    ones = jnp.ones((TOK, LANES), BF)
    sums = jnp.dot(weights, jnp.concatenate([values, ones], axis=1), preferred_element_type=F32)
    total = sums[:, C:]
    scale = 1.0 / total
    logs = top * STEP + jnp.log2(total)
    left = _iota((TOK, LANES), 1) < HEAD
    lane = _iota((TOK, LANES), 1) % SLOT
    packed = jnp.zeros((TOK, LANES), F32)
    for pair in range(HEADS // 2):
        cut = slice(pair * LANES, (pair + 1) * LANES)
        low = slice(2 * pair * TOK, (2 * pair + 1) * TOK)
        high = slice((2 * pair + 1) * TOK, (2 * pair + 2) * TOK)
        out_ref[:, cut] = jnp.where(left, sums[low, cut] * scale[low], sums[high, cut] * scale[high]).astype(BF)
        packed = jnp.where(lane == 2 * pair, logs[low], jnp.where(lane == 2 * pair + 1, logs[high], packed))
    out_ref[:, C:] = _pack_logs(packed)


def _attend(q_pair, k_pair, v_pair, bias):
    rows = q_pair.shape[0]
    left = _iota((rows, LANES), 1) < HEAD
    dims = (((1,), (1,)), ((), ()))
    scores = jnp.concatenate(
        [
            lax.dot_general(q_pair[:, cut], k_pair[:, cut], dims, preferred_element_type=F32)
            for cut in (slice(0, HEAD), slice(HEAD, 2 * HEAD))
        ],
        axis=0,
    )
    if bias is not None:
        scores = scores + bias
    top = jnp.max(scores, axis=1, keepdims=True)
    weights = jnp.exp2((scores - top) * STEP).astype(BF)
    ones = jnp.ones_like(v_pair)
    sums = jnp.dot(weights, jnp.concatenate([v_pair, ones], axis=1), preferred_element_type=F32)
    total = sums[:, LANES:]
    mixed = sums[:, :LANES] / total
    logs = top * STEP + jnp.log2(total)
    return jnp.where(left, mixed[:rows], mixed[rows:]), logs[:rows], logs[rows:]


def _pack_logs(logs):
    first, second, third = _pieces(logs)
    lane = _iota(logs.shape, 1)
    return jnp.where(lane < SLOT, first, jnp.where(lane < 2 * SLOT, second, third)).astype(BF)


def _seat():
    me = lax.axis_index("patch")
    return ((me >> 2) & 3) * 2 + (me & 1)


def _brick():
    me = lax.axis_index("patch")
    return (me >> 4) * 2 + ((me >> 1) & 1)


def query_kernel(
    latent_ref, block_ref, input_ref, query_ref, queries_ref, own_queries_ref, projected_ref, hidden_ref, projected_all, hidden_all
):
    mine = pl.multiple_of(_seat() * TOK, TOK)

    stats = block_ref[:, STATS:, :].reshape(NK * STAT_ROWS, LANES)
    target = _iota((2 * NK, NK * STAT_ROWS), 0)
    source = _iota((2 * NK, NK * STAT_ROWS), 1) - (target % NK) * STAT_ROWS - (target // NK) * 3
    picked = jnp.where((source >= 0) & (source < 3), 1.0, 0.0).astype(BF)
    stats = jnp.dot(picked, stats, preferred_element_type=F32)
    parts_mean, parts_away = stats[:NK], stats[NK:]
    mean = jnp.sum(parts_mean, axis=0, keepdims=True) * (1.0 / NK)
    cell_count = float(QROWS * GROUP)
    away = jnp.sum(parts_away + cell_count * jnp.square(parts_mean - mean), axis=0, keepdims=True)
    gain = lax.rsqrt(away * (1.0 / (cell_count * NK)) + 1e-06)
    spread = jnp.dot(_stack_pieces(mean, gain), _same_group((LANES, C), 1), preferred_element_type=F32)
    which = _iota((16, C), 0)
    center = jnp.sum(jnp.where(which < 3, spread, 0.0), axis=0, keepdims=True)
    gain = jnp.sum(jnp.where(which < 3, 0.0, spread), axis=0, keepdims=True)
    step = QROWS // 2
    starts = range(0, QROWS, step)
    projections = []
    for start in starts:
        cells = latent_ref[start // TOK : (start + step) // TOK].astype(F32).reshape(step, C)
        normed = ((cells - center) * gain).astype(BF)
        projections.append(jnp.dot(normed, input_ref[...], preferred_element_type=F32))
    for start, projected in zip(starts, projections):
        rows = slice(start, start + step)
        projected_all[rows, :] = projected
        row_mean = jnp.mean(projected, axis=1, keepdims=True)
        shifted = projected - row_mean
        row_spread = jnp.mean(jnp.square(shifted), axis=1, keepdims=True)
        hidden = (shifted * lax.rsqrt(row_spread + 1e-05)).astype(BF)
        hidden_all[rows, :] = hidden
        queries_ref[rows, :] = jnp.dot(hidden, query_ref[...], preferred_element_type=F32).astype(BF)
    projected_ref[...] = projected_all[pl.ds(mine, TOK), :]
    hidden_ref[...] = hidden_all[pl.ds(mine, TOK), :]
    own_queries_ref[...] = queries_ref[pl.ds(mine, TOK), :]


def attend_kernel(queries_ref, own_queries_ref, hidden_ref, block_ref, key_ref, value_ref, part_ref, own_ref):
    strips = [block_ref[:, part * TOK : (part + 1) * TOK, :].reshape(KROWS, LANES) for part in range(C // LANES)]
    both_hidden = jnp.concatenate([jnp.concatenate(strips, axis=1), hidden_ref[...]], axis=0)
    pair_proj = jnp.concatenate([key_ref[...], value_ref[...]], axis=1)
    both = jnp.dot(both_hidden, pair_proj, preferred_element_type=F32).astype(BF)
    both_keys, both_values = both[:, :C], both[:, C:]
    keys, fresh_keys = both_keys[:KROWS], both_keys[KROWS:]
    values, fresh_values = both_values[:KROWS], both_values[KROWS:]

    row_band = (_iota((2 * QROWS, KROWS), 0) % QROWS) // TOK
    col_band = _iota((2 * QROWS, KROWS), 1) // TOK
    bias = jnp.where((row_band == _seat()) & (col_band == _brick()), FAR, 0.0).astype(F32)

    lane = _iota((QROWS, LANES), 1) % SLOT
    logs = jnp.zeros((QROWS, LANES), F32)
    for pair in range(HEADS // 2):
        cut = slice(pair * LANES, (pair + 1) * LANES)
        mixed, low, high = _attend(queries_ref[:, cut], keys[:, cut], values[:, cut], bias)
        part_ref[:, :, cut] = mixed.astype(BF).reshape(NQ, TOK, LANES)
        logs = jnp.where(lane == 2 * pair, low, jnp.where(lane == 2 * pair + 1, high, logs))
    part_ref[:, :, C:] = _pack_logs(logs).reshape(NQ, TOK, LANES)
    _attend_own(own_queries_ref[...], fresh_keys, fresh_values, own_ref)


def merge_kernel(part_ref, own_ref, projected_ref, hidden_ref, latent_ref, output_ref, level_ref, next_ref):
    next_ref[...] = hidden_ref[...]
    slot = _iota((LANES, C), 0)
    head = _iota((LANES, C), 1) // HEAD
    spread = jnp.where((slot % SLOT == head) & (slot < 3 * SLOT), 1.0, 0.0).astype(BF)
    logs = jnp.dot(part_ref[:, :, C:].reshape(QROWS, LANES), spread, preferred_element_type=F32)
    logs = logs.reshape(NQ, TOK, C)
    own_logs = jnp.dot(own_ref[:, C:], spread, preferred_element_type=F32)
    top = jnp.maximum(jnp.max(logs, axis=0), own_logs)
    weight = jnp.exp2(own_logs - top)
    total = weight
    mixed = weight * own_ref[:, :C].astype(F32)
    for index in range(NQ):
        weight = jnp.exp2(logs[index] - top)
        total = total + weight
        mixed = mixed + weight * part_ref[index, :, :C].astype(F32)
    attended = (mixed / total).astype(BF)
    out = jnp.dot(attended, output_ref[...], preferred_element_type=F32)
    level = latent_ref[...].reshape(TOK, C).astype(F32) + projected_ref[...] + out
    level_ref[...] = level.astype(BF).reshape(1, TOK, C)


def _call(kernel, out_shape, n_in, scratch=(), limit=16 * 2**20):
    specs = [pl.BlockSpec(memory_space=pltpu.VMEM)] * n_in
    several = isinstance(out_shape, tuple)
    whole = pl.BlockSpec(memory_space=pltpu.VMEM)
    return pl.pallas_call(
        kernel,
        out_shape=out_shape,
        in_specs=specs,
        out_specs=(whole,) * len(out_shape) if several else whole,
        scratch_shapes=list(scratch),
        compiler_params=pltpu.CompilerParams(vmem_limit_bytes=limit),
    )


def _share(block, groups):
    copies = jnp.broadcast_to(block[None], (len(groups[0]),) + block.shape)
    return lax.all_to_all(copies, "patch", 0, 0, axis_index_groups=groups)


def on_device(latent, stale_hidden, input_proj, query_proj, key_proj, value_proj, output_proj):
    shape = jax.ShapeDtypeStruct
    latents = _share(latent.reshape(TOK, C), BRICKS)
    blocks = _call(pack_kernel, shape((NK, STATS + STAT_ROWS, LANES), BF), 2)(latents, stale_hidden)
    blocks = lax.all_to_all(blocks, "patch", 0, 0, axis_index_groups=SEATS)
    queries, own_queries, projected, hidden = _call(
        query_kernel,
        (shape((QROWS, C), BF), shape((TOK, C), BF), shape((TOK, C), F32), shape((TOK, C), BF)),
        4,
        scratch=(pltpu.VMEM((QROWS, C), F32), pltpu.VMEM((QROWS, C), BF)),
    )(latents, blocks, input_proj, query_proj)
    parts, own = _call(attend_kernel, (shape((NQ, TOK, WIDE), BF), shape((TOK, WIDE), BF)), 6)(
        queries, own_queries, hidden, blocks, key_proj, value_proj
    )
    parts = lax.all_to_all(parts, "patch", 0, 0, axis_index_groups=BRICKS)
    return _call(merge_kernel, (shape((1, TOK, C), BF), shape((TOK, C), BF)), 6)(
        parts, own, projected, hidden, latent, output_proj
    )


def solution(mesh):
    rows = P(("batch", "patch"), None)
    return jax.shard_map(
        on_device,
        mesh=mesh,
        in_specs=(P(("batch", "patch"), None, None), rows, P(), P(), P(), P(), P()),
        out_specs=(P(("batch", "patch"), None, None), rows),
        check_vma=False,
    )
```

```python
import math

import jax
import jax.numpy as jnp
from jax import lax
from jax.experimental import pallas as pl
from jax.experimental.pallas import tpu as pltpu
from jax.sharding import PartitionSpec as P

C = 640
HEADS = 10
HEAD = 64
GROUP = 20
TOK = 32
BANDS = 128
LANES = 128
SLOT = 32
WIDE = C + LANES
STATS = TOK * C // LANES
STAT_ROWS = 8
STEP = math.log2(math.e) / math.sqrt(HEAD)
FAR = -1e30

PLACES = [(y, x, z) for y in range(8) for x in range(4) for z in range(4)]


def _groups(key):
    members = {}
    for index, place in enumerate(PLACES):
        members.setdefault(key(*place), []).append(index)
    return [members[k] for k in sorted(members)]


BRICKS = _groups(lambda y, x, z: (y, z // 2))
SEATS = _groups(lambda y, x, z: (x, z % 2))
NQ = len(BRICKS[0])
NK = len(SEATS[0])
QROWS = NQ * TOK
KROWS = NK * TOK
BF = jnp.bfloat16
F32 = jnp.float32


def _iota(shape, axis):
    return lax.broadcasted_iota(jnp.int32, shape, axis)


def _pieces(value):
    first = value.astype(BF).astype(F32)
    rest = value - first
    second = rest.astype(BF).astype(F32)
    return first, second, rest - second


def _same_group(shape, channel_axis):
    group_axis = 1 - channel_axis
    return jnp.where((_iota(shape, channel_axis) * 52429) >> 20 == _iota(shape, group_axis), 1.0, 0.0).astype(BF)


def _stack_pieces(*rows, height=16):
    which = _iota((height, rows[0].shape[1]), 0)
    stacked = jnp.zeros((height, rows[0].shape[1]), F32)
    for index, piece in enumerate(p for row in rows for p in _pieces(row)):
        stacked = jnp.where(which == index, piece, stacked)
    return stacked.astype(BF)


def pack_kernel(latent_ref, stale_ref, out_ref):
    cells = latent_ref[...].astype(F32).reshape(QROWS, C)
    to_group = _same_group((C, LANES), 0)
    to_channel = _same_group((LANES, C), 1)

    def group_sums(row):
        sums = jnp.dot(_stack_pieces(row), to_group, preferred_element_type=F32)
        return jnp.sum(sums, axis=0, keepdims=True)

    pivot = cells[0:1, :]
    shifted = cells - pivot
    total = jnp.sum(shifted, axis=0, keepdims=True)
    mean = pivot + total * (1.0 / QROWS)
    spread = jnp.sum(jnp.square(shifted), axis=0, keepdims=True) - jnp.square(total) * (1.0 / QROWS)
    center = group_sums(mean) * (1.0 / GROUP)
    centers = jnp.dot(_stack_pieces(center), to_channel, preferred_element_type=F32)
    away = group_sums(spread + float(QROWS) * jnp.square(mean - jnp.sum(centers, axis=0, keepdims=True)))
    stats = _stack_pieces(center, away, height=STAT_ROWS)
    for index in range(NK):
        for part in range(C // LANES):
            out_ref[index, part * TOK : (part + 1) * TOK, :] = stale_ref[:, part * LANES : (part + 1) * LANES]
        out_ref[index, STATS:, :] = stats


def _attend_own(queries, keys, values, out_ref):
    head = _iota((TOK, C), 1) // HEAD
    zero = jnp.zeros_like(queries)
    stacked = jnp.concatenate([jnp.where(head == h, queries, zero) for h in range(HEADS)], axis=0)
    scores = lax.dot_general(stacked, keys, (((1,), (1,)), ((), ())), preferred_element_type=F32)
    top = jnp.max(scores, axis=1, keepdims=True)
    weights = jnp.exp2((scores - top) * STEP).astype(BF)
    ones = jnp.ones((TOK, LANES), BF)
    sums = jnp.dot(weights, jnp.concatenate([values, ones], axis=1), preferred_element_type=F32)
    total = sums[:, C:]
    scale = 1.0 / total
    logs = top * STEP + jnp.log2(total)
    left = _iota((TOK, LANES), 1) < HEAD
    lane = _iota((TOK, LANES), 1) % SLOT
    packed = jnp.zeros((TOK, LANES), F32)
    for pair in range(HEADS // 2):
        cut = slice(pair * LANES, (pair + 1) * LANES)
        low = slice(2 * pair * TOK, (2 * pair + 1) * TOK)
        high = slice((2 * pair + 1) * TOK, (2 * pair + 2) * TOK)
        out_ref[:, cut] = jnp.where(left, sums[low, cut] * scale[low], sums[high, cut] * scale[high]).astype(BF)
        packed = jnp.where(lane == 2 * pair, logs[low], jnp.where(lane == 2 * pair + 1, logs[high], packed))
    out_ref[:, C:] = _pack_logs(packed)


def _attend(q_pair, k_pair, v_pair, bias):
    rows = q_pair.shape[0]
    left = _iota((rows, LANES), 1) < HEAD
    dims = (((1,), (1,)), ((), ()))
    scores = jnp.concatenate(
        [
            lax.dot_general(q_pair[:, cut], k_pair[:, cut], dims, preferred_element_type=F32)
            for cut in (slice(0, HEAD), slice(HEAD, 2 * HEAD))
        ],
        axis=0,
    )
    if bias is not None:
        scores = scores + bias
    top = jnp.max(scores, axis=1, keepdims=True)
    weights = jnp.exp2((scores - top) * STEP).astype(BF)
    ones = jnp.ones_like(v_pair)
    sums = jnp.dot(weights, jnp.concatenate([v_pair, ones], axis=1), preferred_element_type=F32)
    total = sums[:, LANES:]
    chosen = jnp.where(left, sums[:rows, :LANES], sums[rows:, :LANES])
    mixed = chosen / jnp.where(left, total[:rows], total[rows:])
    top = top * STEP
    return mixed, (top[:rows], total[:rows]), (top[rows:], total[rows:])


def _pack_logs(logs):
    first, second, third = _pieces(logs)
    lane = _iota(logs.shape, 1)
    return jnp.where(lane < SLOT, first, jnp.where(lane < 2 * SLOT, second, third)).astype(BF)


def _seat():
    me = lax.axis_index("patch")
    return ((me >> 2) & 3) * 2 + (me & 1)


def _brick():
    me = lax.axis_index("patch")
    return (me >> 4) * 2 + ((me >> 1) & 1)


def query_kernel(
    latent_ref, block_ref, input_ref, query_ref, queries_ref, own_queries_ref, projected_ref, hidden_ref, projected_all, hidden_all
):
    mine = pl.multiple_of(_seat() * TOK, TOK)

    stats = block_ref[:, STATS:, :].reshape(NK * STAT_ROWS, LANES)
    target = _iota((2 * NK, NK * STAT_ROWS), 0)
    source = _iota((2 * NK, NK * STAT_ROWS), 1) - (target % NK) * STAT_ROWS - (target // NK) * 3
    picked = jnp.where((source >= 0) & (source < 3), 1.0, 0.0).astype(BF)
    stats = jnp.dot(picked, stats, preferred_element_type=F32)
    parts_mean, parts_away = stats[:NK], stats[NK:]
    mean = jnp.sum(parts_mean, axis=0, keepdims=True) * (1.0 / NK)
    cell_count = float(QROWS * GROUP)
    away = jnp.sum(parts_away + cell_count * jnp.square(parts_mean - mean), axis=0, keepdims=True)
    gain = lax.rsqrt(away * (1.0 / (cell_count * NK)) + 1e-06)
    spread = jnp.dot(_stack_pieces(mean, gain), _same_group((LANES, C), 1), preferred_element_type=F32)
    which = _iota((16, C), 0)
    center = jnp.sum(jnp.where(which < 3, spread, 0.0), axis=0, keepdims=True)
    gain = jnp.sum(jnp.where(which < 3, 0.0, spread), axis=0, keepdims=True)
    step = QROWS // 2
    starts = range(0, QROWS, step)
    projections = []
    for start in starts:
        cells = latent_ref[start // TOK : (start + step) // TOK].astype(F32).reshape(step, C)
        normed = ((cells - center) * gain).astype(BF)
        projections.append(jnp.dot(normed, input_ref[...], preferred_element_type=F32))
    for start, projected in zip(starts, projections):
        rows = slice(start, start + step)
        projected_all[rows, :] = projected
        row_mean = jnp.mean(projected, axis=1, keepdims=True)
        shifted = projected - row_mean
        row_spread = jnp.mean(jnp.square(shifted), axis=1, keepdims=True)
        hidden = (shifted * lax.rsqrt(row_spread + 1e-05)).astype(BF)
        hidden_all[rows, :] = hidden
        queries_ref[rows, :] = jnp.dot(hidden, query_ref[...], preferred_element_type=F32).astype(BF)
    projected_ref[...] = projected_all[pl.ds(mine, TOK), :]
    hidden_ref[...] = hidden_all[pl.ds(mine, TOK), :]
    own_queries_ref[...] = queries_ref[pl.ds(mine, TOK), :]


def attend_kernel(queries_ref, own_queries_ref, hidden_ref, block_ref, key_ref, value_ref, part_ref, own_ref):
    strips = [block_ref[:, part * TOK : (part + 1) * TOK, :].reshape(KROWS, LANES) for part in range(C // LANES)]
    both_hidden = jnp.concatenate([jnp.concatenate(strips, axis=1), hidden_ref[...]], axis=0)
    pair_proj = jnp.concatenate([key_ref[...], value_ref[...]], axis=1)
    both = jnp.dot(both_hidden, pair_proj, preferred_element_type=F32).astype(BF)
    both_keys, both_values = both[:, :C], both[:, C:]
    keys, fresh_keys = both_keys[:KROWS], both_keys[KROWS:]
    values, fresh_values = both_values[:KROWS], both_values[KROWS:]

    row_band = (_iota((2 * QROWS, KROWS), 0) % QROWS) // TOK
    col_band = _iota((2 * QROWS, KROWS), 1) // TOK
    bias = jnp.where((row_band == _seat()) & (col_band == _brick()), FAR, 0.0).astype(F32)

    lane = _iota((QROWS, LANES), 1) % SLOT
    tops = jnp.zeros((QROWS, LANES), F32)
    totals = jnp.ones((QROWS, LANES), F32)
    for pair in range(HEADS // 2):
        cut = slice(pair * LANES, (pair + 1) * LANES)
        mixed, low, high = _attend(queries_ref[:, cut], keys[:, cut], values[:, cut], bias)
        part_ref[:, :, cut] = mixed.astype(BF).reshape(NQ, TOK, LANES)
        first, second = lane == 2 * pair, lane == 2 * pair + 1
        tops = jnp.where(first, low[0], jnp.where(second, high[0], tops))
        totals = jnp.where(first, low[1], jnp.where(second, high[1], totals))
    part_ref[:, :, C:] = _pack_logs(tops + jnp.log2(totals)).reshape(NQ, TOK, LANES)
    _attend_own(own_queries_ref[...], fresh_keys, fresh_values, own_ref)


def merge_kernel(part_ref, own_ref, projected_ref, hidden_ref, latent_ref, output_ref, level_ref, next_ref):
    next_ref[...] = hidden_ref[...]
    slot = _iota((LANES, C), 0)
    head = _iota((LANES, C), 1) // HEAD
    spread = jnp.where((slot % SLOT == head) & (slot < 3 * SLOT), 1.0, 0.0).astype(BF)
    logs = jnp.dot(part_ref[:, :, C:].reshape(QROWS, LANES), spread, preferred_element_type=F32)
    logs = logs.reshape(NQ, TOK, C)
    own_logs = jnp.dot(own_ref[:, C:], spread, preferred_element_type=F32)
    top = jnp.maximum(jnp.max(logs, axis=0), own_logs)
    weight = jnp.exp2(own_logs - top)
    total = weight
    mixed = weight * own_ref[:, :C].astype(F32)
    for index in range(NQ):
        weight = jnp.exp2(logs[index] - top)
        total = total + weight
        mixed = mixed + weight * part_ref[index, :, :C].astype(F32)
    attended = (mixed / total).astype(BF)
    out = jnp.dot(attended, output_ref[...], preferred_element_type=F32)
    level = latent_ref[...].reshape(TOK, C).astype(F32) + projected_ref[...] + out
    level_ref[...] = level.astype(BF).reshape(1, TOK, C)


def _call(kernel, out_shape, n_in, scratch=(), limit=16 * 2**20):
    specs = [pl.BlockSpec(memory_space=pltpu.VMEM)] * n_in
    several = isinstance(out_shape, tuple)
    whole = pl.BlockSpec(memory_space=pltpu.VMEM)
    return pl.pallas_call(
        kernel,
        out_shape=out_shape,
        in_specs=specs,
        out_specs=(whole,) * len(out_shape) if several else whole,
        scratch_shapes=list(scratch),
        compiler_params=pltpu.CompilerParams(vmem_limit_bytes=limit),
    )


def _share(block, groups):
    copies = jnp.broadcast_to(block[None], (len(groups[0]),) + block.shape)
    return lax.all_to_all(copies, "patch", 0, 0, axis_index_groups=groups)


def on_device(latent, stale_hidden, input_proj, query_proj, key_proj, value_proj, output_proj):
    shape = jax.ShapeDtypeStruct
    latents = _share(latent.reshape(TOK, C), BRICKS)
    blocks = _call(pack_kernel, shape((NK, STATS + STAT_ROWS, LANES), BF), 2)(latents, stale_hidden)
    blocks = lax.all_to_all(blocks, "patch", 0, 0, axis_index_groups=SEATS)
    queries, own_queries, projected, hidden = _call(
        query_kernel,
        (shape((QROWS, C), BF), shape((TOK, C), BF), shape((TOK, C), F32), shape((TOK, C), BF)),
        4,
        scratch=(pltpu.VMEM((QROWS, C), F32), pltpu.VMEM((QROWS, C), BF)),
    )(latents, blocks, input_proj, query_proj)
    parts, own = _call(attend_kernel, (shape((NQ, TOK, WIDE), BF), shape((TOK, WIDE), BF)), 6)(
        queries, own_queries, hidden, blocks, key_proj, value_proj
    )
    parts = lax.all_to_all(parts, "patch", 0, 0, axis_index_groups=BRICKS)
    return _call(merge_kernel, (shape((1, TOK, C), BF), shape((TOK, C), BF)), 6)(
        parts, own, projected, hidden, latent, output_proj
    )


def solution(mesh):
    rows = P(("batch", "patch"), None)
    return jax.shard_map(
        on_device,
        mesh=mesh,
        in_specs=(P(("batch", "patch"), None, None), rows, P(), P(), P(), P(), P()),
        out_specs=(P(("batch", "patch"), None, None), rows),
        check_vma=False,
    )
```

```python
import math

import jax
import jax.numpy as jnp
from jax import lax
from jax.experimental import pallas as pl
from jax.experimental.pallas import tpu as pltpu
from jax.sharding import PartitionSpec as P

C = 640
HEADS = 10
HEAD = 64
GROUP = 20
TOK = 32
BANDS = 128
LANES = 128
SLOT = 32
WIDE = C + LANES
STATS = TOK * C // LANES
STAT_ROWS = 8
STEP = math.log2(math.e) / math.sqrt(HEAD)
FAR = -1e30

PLACES = [(y, x, z) for y in range(8) for x in range(4) for z in range(4)]


def _groups(key):
    members = {}
    for index, place in enumerate(PLACES):
        members.setdefault(key(*place), []).append(index)
    return [members[k] for k in sorted(members)]


BRICKS = _groups(lambda y, x, z: (y, z // 2))
SEATS = _groups(lambda y, x, z: (x, z % 2))
NQ = len(BRICKS[0])
NK = len(SEATS[0])
QROWS = NQ * TOK
KROWS = NK * TOK
BF = jnp.bfloat16
F32 = jnp.float32


def _iota(shape, axis):
    return lax.broadcasted_iota(jnp.int32, shape, axis)


def _pieces(value):
    first = value.astype(BF).astype(F32)
    rest = value - first
    second = rest.astype(BF).astype(F32)
    return first, second, rest - second


def _same_group(shape, channel_axis):
    group_axis = 1 - channel_axis
    return jnp.where((_iota(shape, channel_axis) * 52429) >> 20 == _iota(shape, group_axis), 1.0, 0.0).astype(BF)


def _stack_pieces(*rows, height=16):
    which = _iota((height, rows[0].shape[1]), 0)
    stacked = jnp.zeros((height, rows[0].shape[1]), F32)
    for index, piece in enumerate(p for row in rows for p in _pieces(row)):
        stacked = jnp.where(which == index, piece, stacked)
    return stacked.astype(BF)


def pack_kernel(latent_ref, stale_ref, out_ref):
    cells = latent_ref[...].astype(F32).reshape(QROWS, C)
    to_group = _same_group((C, LANES), 0)
    to_channel = _same_group((LANES, C), 1)

    def group_sums(row):
        sums = jnp.dot(_stack_pieces(row), to_group, preferred_element_type=F32)
        return jnp.sum(sums, axis=0, keepdims=True)

    center = group_sums(jnp.sum(cells, axis=0, keepdims=True)) * (1.0 / (QROWS * GROUP))
    centers = jnp.dot(_stack_pieces(center), to_channel, preferred_element_type=F32)
    shifted = cells - jnp.sum(centers, axis=0, keepdims=True)
    away = group_sums(jnp.sum(jnp.square(shifted), axis=0, keepdims=True))
    stats = _stack_pieces(center, away, height=STAT_ROWS)
    for index in range(NK):
        for part in range(C // LANES):
            out_ref[index, part * TOK : (part + 1) * TOK, :] = stale_ref[:, part * LANES : (part + 1) * LANES]
        out_ref[index, STATS:, :] = stats


def _attend_own(queries, keys, values, out_ref):
    head = _iota((TOK, C), 1) // HEAD
    zero = jnp.zeros_like(queries)
    stacked = jnp.concatenate([jnp.where(head == h, queries, zero) for h in range(HEADS)], axis=0)
    scores = lax.dot_general(stacked, keys, (((1,), (1,)), ((), ())), preferred_element_type=F32)
    top = jnp.max(scores, axis=1, keepdims=True)
    weights = jnp.exp2((scores - top) * STEP).astype(BF)
    ones = jnp.ones((TOK, LANES), BF)
    sums = jnp.dot(weights, jnp.concatenate([values, ones], axis=1), preferred_element_type=F32)
    total = sums[:, C:]
    scale = 1.0 / total
    logs = top * STEP + jnp.log2(total)
    left = _iota((TOK, LANES), 1) < HEAD
    lane = _iota((TOK, LANES), 1) % SLOT
    packed = jnp.zeros((TOK, LANES), F32)
    for pair in range(HEADS // 2):
        cut = slice(pair * LANES, (pair + 1) * LANES)
        low = slice(2 * pair * TOK, (2 * pair + 1) * TOK)
        high = slice((2 * pair + 1) * TOK, (2 * pair + 2) * TOK)
        out_ref[:, cut] = jnp.where(left, sums[low, cut] * scale[low], sums[high, cut] * scale[high]).astype(BF)
        packed = jnp.where(lane == 2 * pair, logs[low], jnp.where(lane == 2 * pair + 1, logs[high], packed))
    out_ref[:, C:] = _pack_logs(packed)


def _attend(q_pair, k_pair, v_pair, bias):
    rows = q_pair.shape[0]
    left = _iota((rows, LANES), 1) < HEAD
    dims = (((1,), (1,)), ((), ()))
    scores = jnp.concatenate(
        [
            lax.dot_general(q_pair[:, cut], k_pair[:, cut], dims, preferred_element_type=F32)
            for cut in (slice(0, HEAD), slice(HEAD, 2 * HEAD))
        ],
        axis=0,
    )
    if bias is not None:
        scores = scores + bias
    top = jnp.max(scores, axis=1, keepdims=True)
    weights = jnp.exp2((scores - top) * STEP).astype(BF)
    ones = jnp.ones_like(v_pair)
    sums = jnp.dot(weights, jnp.concatenate([v_pair, ones], axis=1), preferred_element_type=F32)
    total = sums[:, LANES:]
    chosen = jnp.where(left, sums[:rows, :LANES], sums[rows:, :LANES])
    mixed = chosen / jnp.where(left, total[:rows], total[rows:])
    top = top * STEP
    return mixed, (top[:rows], total[:rows]), (top[rows:], total[rows:])


def _pack_logs(logs):
    first, second, third = _pieces(logs)
    lane = _iota(logs.shape, 1)
    return jnp.where(lane < SLOT, first, jnp.where(lane < 2 * SLOT, second, third)).astype(BF)


def _seat():
    me = lax.axis_index("patch")
    return ((me >> 2) & 3) * 2 + (me & 1)


def _brick():
    me = lax.axis_index("patch")
    return (me >> 4) * 2 + ((me >> 1) & 1)


def query_kernel(
    latent_ref, block_ref, input_ref, query_ref, queries_ref, own_queries_ref, projected_ref, hidden_ref, projected_all, hidden_all
):
    mine = pl.multiple_of(_seat() * TOK, TOK)

    stats = block_ref[:, STATS:, :].reshape(NK * STAT_ROWS, LANES)
    target = _iota((2 * NK, NK * STAT_ROWS), 0)
    source = _iota((2 * NK, NK * STAT_ROWS), 1) - (target % NK) * STAT_ROWS - (target // NK) * 3
    picked = jnp.where((source >= 0) & (source < 3), 1.0, 0.0).astype(BF)
    stats = jnp.dot(picked, stats, preferred_element_type=F32)
    parts_mean, parts_away = stats[:NK], stats[NK:]
    mean = jnp.sum(parts_mean, axis=0, keepdims=True) * (1.0 / NK)
    cell_count = float(QROWS * GROUP)
    away = jnp.sum(parts_away + cell_count * jnp.square(parts_mean - mean), axis=0, keepdims=True)
    gain = lax.rsqrt(away * (1.0 / (cell_count * NK)) + 1e-06)
    spread = jnp.dot(_stack_pieces(mean, gain), _same_group((LANES, C), 1), preferred_element_type=F32)
    which = _iota((16, C), 0)
    center = jnp.sum(jnp.where(which < 3, spread, 0.0), axis=0, keepdims=True)
    gain = jnp.sum(jnp.where(which < 3, 0.0, spread), axis=0, keepdims=True)
    step = QROWS // 2
    starts = range(0, QROWS, step)
    projections = []
    for start in starts:
        cells = latent_ref[start // TOK : (start + step) // TOK].astype(F32).reshape(step, C)
        normed = ((cells - center) * gain).astype(BF)
        projections.append(jnp.dot(normed, input_ref[...], preferred_element_type=F32))
    for start, projected in zip(starts, projections):
        rows = slice(start, start + step)
        projected_all[rows, :] = projected
        row_mean = jnp.mean(projected, axis=1, keepdims=True)
        shifted = projected - row_mean
        row_spread = jnp.mean(jnp.square(shifted), axis=1, keepdims=True)
        hidden = (shifted * lax.rsqrt(row_spread + 1e-05)).astype(BF)
        hidden_all[rows, :] = hidden
        queries_ref[rows, :] = jnp.dot(hidden, query_ref[...], preferred_element_type=F32).astype(BF)
    projected_ref[...] = projected_all[pl.ds(mine, TOK), :]
    hidden_ref[...] = hidden_all[pl.ds(mine, TOK), :]
    own_queries_ref[...] = queries_ref[pl.ds(mine, TOK), :]


def attend_kernel(queries_ref, own_queries_ref, hidden_ref, block_ref, key_ref, value_ref, part_ref, own_ref):
    strips = [block_ref[:, part * TOK : (part + 1) * TOK, :].reshape(KROWS, LANES) for part in range(C // LANES)]
    both_hidden = jnp.concatenate([jnp.concatenate(strips, axis=1), hidden_ref[...]], axis=0)
    pair_proj = jnp.concatenate([key_ref[...], value_ref[...]], axis=1)
    both = jnp.dot(both_hidden, pair_proj, preferred_element_type=F32).astype(BF)
    both_keys, both_values = both[:, :C], both[:, C:]
    keys, fresh_keys = both_keys[:KROWS], both_keys[KROWS:]
    values, fresh_values = both_values[:KROWS], both_values[KROWS:]

    row_band = (_iota((2 * QROWS, KROWS), 0) % QROWS) // TOK
    col_band = _iota((2 * QROWS, KROWS), 1) // TOK
    bias = jnp.where((row_band == _seat()) & (col_band == _brick()), FAR, 0.0).astype(F32)

    lane = _iota((QROWS, LANES), 1) % SLOT
    tops = jnp.zeros((QROWS, LANES), F32)
    totals = jnp.ones((QROWS, LANES), F32)
    for pair in range(HEADS // 2):
        cut = slice(pair * LANES, (pair + 1) * LANES)
        mixed, low, high = _attend(queries_ref[:, cut], keys[:, cut], values[:, cut], bias)
        part_ref[:, :, cut] = mixed.astype(BF).reshape(NQ, TOK, LANES)
        first, second = lane == 2 * pair, lane == 2 * pair + 1
        tops = jnp.where(first, low[0], jnp.where(second, high[0], tops))
        totals = jnp.where(first, low[1], jnp.where(second, high[1], totals))
    part_ref[:, :, C:] = _pack_logs(tops + jnp.log2(totals)).reshape(NQ, TOK, LANES)
    _attend_own(own_queries_ref[...], fresh_keys, fresh_values, own_ref)


def merge_kernel(part_ref, own_ref, projected_ref, hidden_ref, latent_ref, output_ref, level_ref, next_ref):
    next_ref[...] = hidden_ref[...]
    slot = _iota((LANES, C), 0)
    head = _iota((LANES, C), 1) // HEAD
    spread = jnp.where((slot % SLOT == head) & (slot < 3 * SLOT), 1.0, 0.0).astype(BF)
    logs = jnp.dot(part_ref[:, :, C:].reshape(QROWS, LANES), spread, preferred_element_type=F32)
    logs = logs.reshape(NQ, TOK, C)
    own_logs = jnp.dot(own_ref[:, C:], spread, preferred_element_type=F32)
    top = jnp.maximum(jnp.max(logs, axis=0), own_logs)
    weight = jnp.exp2(own_logs - top)
    total = weight
    mixed = weight * own_ref[:, :C].astype(F32)
    for index in range(NQ):
        weight = jnp.exp2(logs[index] - top)
        total = total + weight
        mixed = mixed + weight * part_ref[index, :, :C].astype(F32)
    attended = (mixed / total).astype(BF)
    out = jnp.dot(attended, output_ref[...], preferred_element_type=F32)
    level = latent_ref[...].reshape(TOK, C).astype(F32) + projected_ref[...] + out
    level_ref[...] = level.astype(BF).reshape(1, TOK, C)


def _call(kernel, out_shape, n_in, scratch=(), limit=16 * 2**20):
    specs = [pl.BlockSpec(memory_space=pltpu.VMEM)] * n_in
    several = isinstance(out_shape, tuple)
    whole = pl.BlockSpec(memory_space=pltpu.VMEM)
    return pl.pallas_call(
        kernel,
        out_shape=out_shape,
        in_specs=specs,
        out_specs=(whole,) * len(out_shape) if several else whole,
        scratch_shapes=list(scratch),
        compiler_params=pltpu.CompilerParams(vmem_limit_bytes=limit),
    )


def _share(block, groups):
    copies = jnp.broadcast_to(block[None], (len(groups[0]),) + block.shape)
    return lax.all_to_all(copies, "patch", 0, 0, axis_index_groups=groups)


def on_device(latent, stale_hidden, input_proj, query_proj, key_proj, value_proj, output_proj):
    shape = jax.ShapeDtypeStruct
    latents = _share(latent.reshape(TOK, C), BRICKS)
    blocks = _call(pack_kernel, shape((NK, STATS + STAT_ROWS, LANES), BF), 2)(latents, stale_hidden)
    blocks = lax.all_to_all(blocks, "patch", 0, 0, axis_index_groups=SEATS)
    queries, own_queries, projected, hidden = _call(
        query_kernel,
        (shape((QROWS, C), BF), shape((TOK, C), BF), shape((TOK, C), F32), shape((TOK, C), BF)),
        4,
        scratch=(pltpu.VMEM((QROWS, C), F32), pltpu.VMEM((QROWS, C), BF)),
    )(latents, blocks, input_proj, query_proj)
    parts, own = _call(attend_kernel, (shape((NQ, TOK, WIDE), BF), shape((TOK, WIDE), BF)), 6)(
        queries, own_queries, hidden, blocks, key_proj, value_proj
    )
    parts = lax.all_to_all(parts, "patch", 0, 0, axis_index_groups=BRICKS)
    return _call(merge_kernel, (shape((1, TOK, C), BF), shape((TOK, C), BF)), 6)(
        parts, own, projected, hidden, latent, output_proj
    )


def solution(mesh):
    rows = P(("batch", "patch"), None)
    return jax.shard_map(
        on_device,
        mesh=mesh,
        in_specs=(P(("batch", "patch"), None, None), rows, P(), P(), P(), P(), P()),
        out_specs=(P(("batch", "patch"), None, None), rows),
        check_vma=False,
    )
```

```python
import math

import jax
import jax.numpy as jnp
from jax import lax
from jax.experimental import pallas as pl
from jax.experimental.pallas import tpu as pltpu
from jax.sharding import PartitionSpec as P

C = 640
HEADS = 10
HEAD = 64
GROUP = 20
TOK = 32
BANDS = 128
LANES = 128
SLOT = 32
WIDE = C + LANES
STATS = TOK * C // LANES
STAT_ROWS = 8
STEP = math.log2(math.e) / math.sqrt(HEAD)
FAR = -1e30

PLACES = [(y, x, z) for y in range(8) for x in range(4) for z in range(4)]


def _groups(key):
    members = {}
    for index, place in enumerate(PLACES):
        members.setdefault(key(*place), []).append(index)
    return [members[k] for k in sorted(members)]


BRICKS = _groups(lambda y, x, z: (y, z // 2))
SEATS = _groups(lambda y, x, z: (x, z % 2))
NQ = len(BRICKS[0])
NK = len(SEATS[0])
QROWS = NQ * TOK
KROWS = NK * TOK
BF = jnp.bfloat16
F32 = jnp.float32


def _iota(shape, axis):
    return lax.broadcasted_iota(jnp.int32, shape, axis)


def _pieces(value):
    first = value.astype(BF).astype(F32)
    rest = value - first
    second = rest.astype(BF).astype(F32)
    return first, second, rest - second


def _same_group(shape, channel_axis):
    group_axis = 1 - channel_axis
    return jnp.where((_iota(shape, channel_axis) * 52429) >> 20 == _iota(shape, group_axis), 1.0, 0.0).astype(BF)


def _stack_pieces(*rows, height=16):
    which = _iota((height, rows[0].shape[1]), 0)
    stacked = jnp.zeros((height, rows[0].shape[1]), F32)
    for index, piece in enumerate(p for row in rows for p in _pieces(row)):
        stacked = jnp.where(which == index, piece, stacked)
    return stacked.astype(BF)


def pack_kernel(latent_ref, stale_ref, out_ref):
    cells = latent_ref[...].astype(F32).reshape(QROWS, C)
    to_group = _same_group((C, LANES), 0)
    to_channel = _same_group((LANES, C), 1)

    def group_sums(row):
        sums = jnp.dot(_stack_pieces(row), to_group, preferred_element_type=F32)
        return jnp.sum(sums, axis=0, keepdims=True)

    mean = jnp.sum(cells, axis=0, keepdims=True) * (1.0 / QROWS)
    spread = jnp.sum(jnp.square(cells - mean), axis=0, keepdims=True)
    center = group_sums(mean) * (1.0 / GROUP)
    centers = jnp.dot(_stack_pieces(center), to_channel, preferred_element_type=F32)
    away = group_sums(spread + float(QROWS) * jnp.square(mean - jnp.sum(centers, axis=0, keepdims=True)))
    stats = _stack_pieces(center, away, height=STAT_ROWS)
    for index in range(NK):
        for part in range(C // LANES):
            out_ref[index, part * TOK : (part + 1) * TOK, :] = stale_ref[:, part * LANES : (part + 1) * LANES]
        out_ref[index, STATS:, :] = stats


def _attend_own(queries, keys, values, out_ref):
    head = _iota((TOK, C), 1) // HEAD
    zero = jnp.zeros_like(queries)
    stacked = jnp.concatenate([jnp.where(head == h, queries, zero) for h in range(HEADS)], axis=0)
    scores = lax.dot_general(stacked, keys, (((1,), (1,)), ((), ())), preferred_element_type=F32)
    top = jnp.max(scores, axis=1, keepdims=True)
    weights = jnp.exp2((scores - top) * STEP).astype(BF)
    ones = jnp.ones((TOK, LANES), BF)
    sums = jnp.dot(weights, jnp.concatenate([values, ones], axis=1), preferred_element_type=F32)
    total = sums[:, C:]
    scale = 1.0 / total
    logs = top * STEP + jnp.log2(total)
    left = _iota((TOK, LANES), 1) < HEAD
    lane = _iota((TOK, LANES), 1) % SLOT
    packed = jnp.zeros((TOK, LANES), F32)
    for pair in range(HEADS // 2):
        cut = slice(pair * LANES, (pair + 1) * LANES)
        low = slice(2 * pair * TOK, (2 * pair + 1) * TOK)
        high = slice((2 * pair + 1) * TOK, (2 * pair + 2) * TOK)
        out_ref[:, cut] = jnp.where(left, sums[low, cut] * scale[low], sums[high, cut] * scale[high]).astype(BF)
        packed = jnp.where(lane == 2 * pair, logs[low], jnp.where(lane == 2 * pair + 1, logs[high], packed))
    out_ref[:, C:] = _pack_logs(packed)


def _attend(q_pair, k_pair, v_pair, bias):
    rows = q_pair.shape[0]
    left = _iota((rows, LANES), 1) < HEAD
    dims = (((1,), (1,)), ((), ()))
    scores = jnp.concatenate(
        [
            lax.dot_general(q_pair[:, cut], k_pair[:, cut], dims, preferred_element_type=F32)
            for cut in (slice(0, HEAD), slice(HEAD, 2 * HEAD))
        ],
        axis=0,
    )
    if bias is not None:
        scores = scores + bias
    top = jnp.max(scores, axis=1, keepdims=True)
    weights = jnp.exp2((scores - top) * STEP).astype(BF)
    ones = jnp.ones_like(v_pair)
    sums = jnp.dot(weights, jnp.concatenate([v_pair, ones], axis=1), preferred_element_type=F32)
    total = sums[:, LANES:]
    chosen = jnp.where(left, sums[:rows, :LANES], sums[rows:, :LANES])
    mixed = chosen / jnp.where(left, total[:rows], total[rows:])
    top = top * STEP
    return mixed, (top[:rows], total[:rows]), (top[rows:], total[rows:])


def _pack_logs(logs):
    first, second, third = _pieces(logs)
    lane = _iota(logs.shape, 1)
    return jnp.where(lane < SLOT, first, jnp.where(lane < 2 * SLOT, second, third)).astype(BF)


def _seat():
    me = lax.axis_index("patch")
    return ((me >> 2) & 3) * 2 + (me & 1)


def _brick():
    me = lax.axis_index("patch")
    return (me >> 4) * 2 + ((me >> 1) & 1)


def query_kernel(
    latent_ref, block_ref, input_ref, query_ref, queries_ref, own_queries_ref, projected_ref, hidden_ref, projected_all, hidden_all
):
    mine = pl.multiple_of(_seat() * TOK, TOK)

    stats = block_ref[:, STATS:, :].reshape(NK * STAT_ROWS, LANES)
    target = _iota((2 * NK, NK * STAT_ROWS), 0)
    source = _iota((2 * NK, NK * STAT_ROWS), 1) - (target % NK) * STAT_ROWS - (target // NK) * 3
    picked = jnp.where((source >= 0) & (source < 3), 1.0, 0.0).astype(BF)
    stats = jnp.dot(picked, stats, preferred_element_type=F32)
    parts_mean, parts_away = stats[:NK], stats[NK:]
    mean = jnp.sum(parts_mean, axis=0, keepdims=True) * (1.0 / NK)
    cell_count = float(QROWS * GROUP)
    away = jnp.sum(parts_away + cell_count * jnp.square(parts_mean - mean), axis=0, keepdims=True)
    gain = lax.rsqrt(away * (1.0 / (cell_count * NK)) + 1e-06)
    spread = jnp.dot(_stack_pieces(mean, gain), _same_group((LANES, C), 1), preferred_element_type=F32)
    which = _iota((16, C), 0)
    center = jnp.sum(jnp.where(which < 3, spread, 0.0), axis=0, keepdims=True)
    gain = jnp.sum(jnp.where(which < 3, 0.0, spread), axis=0, keepdims=True)
    step = QROWS // 2
    starts = range(0, QROWS, step)
    projections = []
    for start in starts:
        cells = latent_ref[start // TOK : (start + step) // TOK].astype(F32).reshape(step, C)
        normed = ((cells - center) * gain).astype(BF)
        projections.append(jnp.dot(normed, input_ref[...], preferred_element_type=F32))
    for start, projected in zip(starts, projections):
        rows = slice(start, start + step)
        projected_all[rows, :] = projected
        row_mean = jnp.mean(projected, axis=1, keepdims=True)
        shifted = projected - row_mean
        row_spread = jnp.mean(jnp.square(shifted), axis=1, keepdims=True)
        hidden = (shifted * lax.rsqrt(row_spread + 1e-05)).astype(BF)
        hidden_all[rows, :] = hidden
        queries_ref[rows, :] = jnp.dot(hidden, query_ref[...], preferred_element_type=F32).astype(BF)
    projected_ref[...] = projected_all[pl.ds(mine, TOK), :]
    hidden_ref[...] = hidden_all[pl.ds(mine, TOK), :]
    own_queries_ref[...] = queries_ref[pl.ds(mine, TOK), :]


def attend_kernel(queries_ref, own_queries_ref, hidden_ref, block_ref, key_ref, value_ref, part_ref, own_ref):
    strips = [block_ref[:, part * TOK : (part + 1) * TOK, :].reshape(KROWS, LANES) for part in range(C // LANES)]
    both_hidden = jnp.concatenate([jnp.concatenate(strips, axis=1), hidden_ref[...]], axis=0)
    pair_proj = jnp.concatenate([key_ref[...], value_ref[...]], axis=1)
    both = jnp.dot(both_hidden, pair_proj, preferred_element_type=F32).astype(BF)
    both_keys, both_values = both[:, :C], both[:, C:]
    keys, fresh_keys = both_keys[:KROWS], both_keys[KROWS:]
    values, fresh_values = both_values[:KROWS], both_values[KROWS:]

    row_band = (_iota((2 * QROWS, KROWS), 0) % QROWS) // TOK
    col_band = _iota((2 * QROWS, KROWS), 1) // TOK
    bias = jnp.where((row_band == _seat()) & (col_band == _brick()), FAR, 0.0).astype(F32)

    lane = _iota((QROWS, LANES), 1) % SLOT
    tops = jnp.zeros((QROWS, LANES), F32)
    totals = jnp.ones((QROWS, LANES), F32)
    for pair in range(HEADS // 2):
        cut = slice(pair * LANES, (pair + 1) * LANES)
        mixed, low, high = _attend(queries_ref[:, cut], keys[:, cut], values[:, cut], bias)
        part_ref[:, :, cut] = mixed.astype(BF).reshape(NQ, TOK, LANES)
        first, second = lane == 2 * pair, lane == 2 * pair + 1
        tops = jnp.where(first, low[0], jnp.where(second, high[0], tops))
        totals = jnp.where(first, low[1], jnp.where(second, high[1], totals))
    part_ref[:, :, C:] = _pack_logs(tops + jnp.log2(totals)).reshape(NQ, TOK, LANES)
    _attend_own(own_queries_ref[...], fresh_keys, fresh_values, own_ref)


def merge_kernel(part_ref, own_ref, projected_ref, hidden_ref, latent_ref, output_ref, level_ref, next_ref):
    next_ref[...] = hidden_ref[...]
    slot = _iota((LANES, C), 0)
    head = _iota((LANES, C), 1) // HEAD
    spread = jnp.where((slot % SLOT == head) & (slot < 3 * SLOT), 1.0, 0.0).astype(BF)
    logs = jnp.dot(part_ref[:, :, C:].reshape(QROWS, LANES), spread, preferred_element_type=F32)
    logs = logs.reshape(NQ, TOK, C)
    own_logs = jnp.dot(own_ref[:, C:], spread, preferred_element_type=F32)
    top = jnp.maximum(jnp.max(logs, axis=0), own_logs)
    weight = jnp.exp2(own_logs - top)
    total = weight
    mixed = weight * own_ref[:, :C].astype(F32)
    for index in range(NQ):
        weight = jnp.exp2(logs[index] - top)
        total = total + weight
        mixed = mixed + weight * part_ref[index, :, :C].astype(F32)
    attended = (mixed / total).astype(BF)
    out = jnp.dot(attended, output_ref[...], preferred_element_type=F32)
    level = latent_ref[...].reshape(TOK, C).astype(F32) + projected_ref[...] + out
    level_ref[...] = level.astype(BF).reshape(1, TOK, C)


def _call(kernel, out_shape, n_in, scratch=(), limit=16 * 2**20):
    specs = [pl.BlockSpec(memory_space=pltpu.VMEM)] * n_in
    several = isinstance(out_shape, tuple)
    whole = pl.BlockSpec(memory_space=pltpu.VMEM)
    return pl.pallas_call(
        kernel,
        out_shape=out_shape,
        in_specs=specs,
        out_specs=(whole,) * len(out_shape) if several else whole,
        scratch_shapes=list(scratch),
        compiler_params=pltpu.CompilerParams(vmem_limit_bytes=limit),
    )


def _share(block, groups):
    copies = jnp.broadcast_to(block[None], (len(groups[0]),) + block.shape)
    return lax.all_to_all(copies, "patch", 0, 0, axis_index_groups=groups)


def on_device(latent, stale_hidden, input_proj, query_proj, key_proj, value_proj, output_proj):
    shape = jax.ShapeDtypeStruct
    latents = _share(latent.reshape(TOK, C), BRICKS)
    blocks = _call(pack_kernel, shape((NK, STATS + STAT_ROWS, LANES), BF), 2)(latents, stale_hidden)
    blocks = lax.all_to_all(blocks, "patch", 0, 0, axis_index_groups=SEATS)
    queries, own_queries, projected, hidden = _call(
        query_kernel,
        (shape((QROWS, C), BF), shape((TOK, C), BF), shape((TOK, C), F32), shape((TOK, C), BF)),
        4,
        scratch=(pltpu.VMEM((QROWS, C), F32), pltpu.VMEM((QROWS, C), BF)),
    )(latents, blocks, input_proj, query_proj)
    parts, own = _call(attend_kernel, (shape((NQ, TOK, WIDE), BF), shape((TOK, WIDE), BF)), 6)(
        queries, own_queries, hidden, blocks, key_proj, value_proj
    )
    parts = lax.all_to_all(parts, "patch", 0, 0, axis_index_groups=BRICKS)
    return _call(merge_kernel, (shape((1, TOK, C), BF), shape((TOK, C), BF)), 6)(
        parts, own, projected, hidden, latent, output_proj
    )


def solution(mesh):
    rows = P(("batch", "patch"), None)
    return jax.shard_map(
        on_device,
        mesh=mesh,
        in_specs=(P(("batch", "patch"), None, None), rows, P(), P(), P(), P(), P()),
        out_specs=(P(("batch", "patch"), None, None), rows),
        check_vma=False,
    )
```

```python
import math

import jax
import jax.numpy as jnp
from jax import lax
from jax.experimental import pallas as pl
from jax.experimental.pallas import tpu as pltpu
from jax.sharding import PartitionSpec as P

C = 640
HEADS = 10
HEAD = 64
GROUP = 20
TOK = 32
BANDS = 128
LANES = 128
SLOT = 32
WIDE = C + LANES
STATS = TOK * C // LANES
STAT_ROWS = 8
STEP = math.log2(math.e) / math.sqrt(HEAD)
FAR = -1e30

PLACES = [(y, x, z) for y in range(8) for x in range(4) for z in range(4)]


def _groups(key):
    members = {}
    for index, place in enumerate(PLACES):
        members.setdefault(key(*place), []).append(index)
    return [members[k] for k in sorted(members)]


BRICKS = _groups(lambda y, x, z: (y, z // 2))
SEATS = [sorted(group, key=lambda index: (index % 4, index)) for group in _groups(lambda y, x, z: (x, z % 2))]
NQ = len(BRICKS[0])
NK = len(SEATS[0])
QROWS = NQ * TOK
KROWS = NK * TOK
BF = jnp.bfloat16
F32 = jnp.float32


def _iota(shape, axis):
    return lax.broadcasted_iota(jnp.int32, shape, axis)


def _pieces(value):
    first = value.astype(BF).astype(F32)
    rest = value - first
    second = rest.astype(BF).astype(F32)
    return first, second, rest - second


def _same_group(shape, channel_axis):
    group_axis = 1 - channel_axis
    return jnp.where((_iota(shape, channel_axis) * 52429) >> 20 == _iota(shape, group_axis), 1.0, 0.0).astype(BF)


def _stack_pieces(*rows, height=16):
    which = _iota((height, rows[0].shape[1]), 0)
    stacked = jnp.zeros((height, rows[0].shape[1]), F32)
    for index, piece in enumerate(p for row in rows for p in _pieces(row)):
        stacked = jnp.where(which == index, piece, stacked)
    return stacked.astype(BF)


def pack_kernel(latent_ref, stale_ref, out_ref):
    cells = latent_ref[...].astype(F32).reshape(QROWS, C)
    to_group = _same_group((C, LANES), 0)
    to_channel = _same_group((LANES, C), 1)

    def group_sums(row):
        sums = jnp.dot(_stack_pieces(row), to_group, preferred_element_type=F32)
        return jnp.sum(sums, axis=0, keepdims=True)

    center = group_sums(jnp.sum(cells, axis=0, keepdims=True)) * (1.0 / (QROWS * GROUP))
    centers = jnp.dot(_stack_pieces(center), to_channel, preferred_element_type=F32)
    shifted = cells - jnp.sum(centers, axis=0, keepdims=True)
    away = group_sums(jnp.sum(jnp.square(shifted), axis=0, keepdims=True))
    stats = _stack_pieces(center, away, height=STAT_ROWS)
    for index in range(NK):
        for part in range(C // LANES):
            out_ref[index, part * TOK : (part + 1) * TOK, :] = stale_ref[:, part * LANES : (part + 1) * LANES]
        out_ref[index, STATS:, :] = stats


def _attend_own(queries, keys, values, out_ref):
    head = _iota((TOK, C), 1) // HEAD
    zero = jnp.zeros_like(queries)
    stacked = jnp.concatenate([jnp.where(head == h, queries, zero) for h in range(HEADS)], axis=0)
    scores = lax.dot_general(stacked, keys, (((1,), (1,)), ((), ())), preferred_element_type=F32)
    top = jnp.max(scores, axis=1, keepdims=True)
    weights = jnp.exp2((scores - top) * STEP).astype(BF)
    ones = jnp.ones((TOK, LANES), BF)
    sums = jnp.dot(weights, jnp.concatenate([values, ones], axis=1), preferred_element_type=F32)
    total = sums[:, C:]
    scale = 1.0 / total
    logs = top * STEP + jnp.log2(total)
    left = _iota((TOK, LANES), 1) < HEAD
    lane = _iota((TOK, LANES), 1) % SLOT
    packed = jnp.zeros((TOK, LANES), F32)
    for pair in range(HEADS // 2):
        cut = slice(pair * LANES, (pair + 1) * LANES)
        low = slice(2 * pair * TOK, (2 * pair + 1) * TOK)
        high = slice((2 * pair + 1) * TOK, (2 * pair + 2) * TOK)
        out_ref[:, cut] = jnp.where(left, sums[low, cut] * scale[low], sums[high, cut] * scale[high]).astype(BF)
        packed = jnp.where(lane == 2 * pair, logs[low], jnp.where(lane == 2 * pair + 1, logs[high], packed))
    out_ref[:, C:] = _pack_logs(packed)


def _attend(q_pair, k_pair, v_pair, bias):
    rows = q_pair.shape[0]
    left = _iota((rows, LANES), 1) < HEAD
    dims = (((1,), (1,)), ((), ()))
    scores = jnp.concatenate(
        [
            lax.dot_general(q_pair[:, cut], k_pair[:, cut], dims, preferred_element_type=F32)
            for cut in (slice(0, HEAD), slice(HEAD, 2 * HEAD))
        ],
        axis=0,
    )
    if bias is not None:
        scores = scores + bias
    top = jnp.max(scores, axis=1, keepdims=True)
    weights = jnp.exp2((scores - top) * STEP).astype(BF)
    ones = jnp.ones_like(v_pair)
    sums = jnp.dot(weights, jnp.concatenate([v_pair, ones], axis=1), preferred_element_type=F32)
    total = sums[:, LANES:]
    chosen = jnp.where(left, sums[:rows, :LANES], sums[rows:, :LANES])
    mixed = chosen / jnp.where(left, total[:rows], total[rows:])
    top = top * STEP
    return mixed, (top[:rows], total[:rows]), (top[rows:], total[rows:])


def _pack_logs(logs):
    first, second, third = _pieces(logs)
    lane = _iota(logs.shape, 1)
    return jnp.where(lane < SLOT, first, jnp.where(lane < 2 * SLOT, second, third)).astype(BF)


def _seat():
    me = lax.axis_index("patch")
    return ((me >> 2) & 3) * 2 + (me & 1)


def _brick():
    me = lax.axis_index("patch")
    return ((me >> 1) & 1) * 8 + (me >> 4)


def query_kernel(
    latent_ref, block_ref, input_ref, query_ref, queries_ref, own_queries_ref, projected_ref, hidden_ref, projected_all, hidden_all
):
    mine = pl.multiple_of(_seat() * TOK, TOK)

    stats = block_ref[:, STATS:, :].reshape(NK * STAT_ROWS, LANES)
    target = _iota((2 * NK, NK * STAT_ROWS), 0)
    source = _iota((2 * NK, NK * STAT_ROWS), 1) - (target % NK) * STAT_ROWS - (target // NK) * 3
    picked = jnp.where((source >= 0) & (source < 3), 1.0, 0.0).astype(BF)
    stats = jnp.dot(picked, stats, preferred_element_type=F32)
    parts_mean, parts_away = stats[:NK], stats[NK:]
    mean = jnp.sum(parts_mean, axis=0, keepdims=True) * (1.0 / NK)
    cell_count = float(QROWS * GROUP)
    away = jnp.sum(parts_away + cell_count * jnp.square(parts_mean - mean), axis=0, keepdims=True)
    gain = lax.rsqrt(away * (1.0 / (cell_count * NK)) + 1e-06)
    spread = jnp.dot(_stack_pieces(mean, gain), _same_group((LANES, C), 1), preferred_element_type=F32)
    which = _iota((16, C), 0)
    center = jnp.sum(jnp.where(which < 3, spread, 0.0), axis=0, keepdims=True)
    gain = jnp.sum(jnp.where(which < 3, 0.0, spread), axis=0, keepdims=True)
    step = QROWS // 2
    starts = range(0, QROWS, step)
    projections = []
    for start in starts:
        cells = latent_ref[start // TOK : (start + step) // TOK].astype(F32).reshape(step, C)
        normed = ((cells - center) * gain).astype(BF)
        projections.append(jnp.dot(normed, input_ref[...], preferred_element_type=F32))
    for start, projected in zip(starts, projections):
        rows = slice(start, start + step)
        projected_all[rows, :] = projected
        row_mean = jnp.mean(projected, axis=1, keepdims=True)
        shifted = projected - row_mean
        row_spread = jnp.mean(jnp.square(shifted), axis=1, keepdims=True)
        hidden = (shifted * lax.rsqrt(row_spread + 1e-05)).astype(BF)
        hidden_all[rows, :] = hidden
        queries_ref[rows, :] = jnp.dot(hidden, query_ref[...], preferred_element_type=F32).astype(BF)
    projected_ref[...] = projected_all[pl.ds(mine, TOK), :]
    hidden_ref[...] = hidden_all[pl.ds(mine, TOK), :]
    own_queries_ref[...] = queries_ref[pl.ds(mine, TOK), :]


def attend_kernel(queries_ref, own_queries_ref, hidden_ref, block_ref, key_ref, value_ref, part_ref, own_ref):
    strips = [block_ref[:, part * TOK : (part + 1) * TOK, :].reshape(KROWS, LANES) for part in range(C // LANES)]
    both_hidden = jnp.concatenate([jnp.concatenate(strips, axis=1), hidden_ref[...]], axis=0)
    pair_proj = jnp.concatenate([key_ref[...], value_ref[...]], axis=1)
    both = jnp.dot(both_hidden, pair_proj, preferred_element_type=F32).astype(BF)
    both_keys, both_values = both[:, :C], both[:, C:]
    keys, fresh_keys = both_keys[:KROWS], both_keys[KROWS:]
    values, fresh_values = both_values[:KROWS], both_values[KROWS:]

    row_band = (_iota((2 * QROWS, KROWS), 0) % QROWS) // TOK
    col_band = _iota((2 * QROWS, KROWS), 1) // TOK
    bias = jnp.where((row_band == _seat()) & (col_band == _brick()), FAR, 0.0).astype(F32)

    lane = _iota((QROWS, LANES), 1) % SLOT
    tops = jnp.zeros((QROWS, LANES), F32)
    totals = jnp.ones((QROWS, LANES), F32)
    for pair in range(HEADS // 2):
        cut = slice(pair * LANES, (pair + 1) * LANES)
        mixed, low, high = _attend(queries_ref[:, cut], keys[:, cut], values[:, cut], bias)
        part_ref[:, :, cut] = mixed.astype(BF).reshape(NQ, TOK, LANES)
        first, second = lane == 2 * pair, lane == 2 * pair + 1
        tops = jnp.where(first, low[0], jnp.where(second, high[0], tops))
        totals = jnp.where(first, low[1], jnp.where(second, high[1], totals))
    part_ref[:, :, C:] = _pack_logs(tops + jnp.log2(totals)).reshape(NQ, TOK, LANES)
    _attend_own(own_queries_ref[...], fresh_keys, fresh_values, own_ref)


def merge_kernel(part_ref, own_ref, projected_ref, hidden_ref, latent_ref, output_ref, level_ref, next_ref):
    next_ref[...] = hidden_ref[...]
    slot = _iota((LANES, C), 0)
    head = _iota((LANES, C), 1) // HEAD
    spread = jnp.where((slot % SLOT == head) & (slot < 3 * SLOT), 1.0, 0.0).astype(BF)
    logs = jnp.dot(part_ref[:, :, C:].reshape(QROWS, LANES), spread, preferred_element_type=F32)
    logs = logs.reshape(NQ, TOK, C)
    own_logs = jnp.dot(own_ref[:, C:], spread, preferred_element_type=F32)
    top = jnp.maximum(jnp.max(logs, axis=0), own_logs)
    weight = jnp.exp2(own_logs - top)
    total = weight
    mixed = weight * own_ref[:, :C].astype(F32)
    for index in range(NQ):
        weight = jnp.exp2(logs[index] - top)
        total = total + weight
        mixed = mixed + weight * part_ref[index, :, :C].astype(F32)
    attended = (mixed / total).astype(BF)
    out = jnp.dot(attended, output_ref[...], preferred_element_type=F32)
    level = latent_ref[...].reshape(TOK, C).astype(F32) + projected_ref[...] + out
    level_ref[...] = level.astype(BF).reshape(1, TOK, C)


def _call(kernel, out_shape, n_in, scratch=(), limit=16 * 2**20):
    specs = [pl.BlockSpec(memory_space=pltpu.VMEM)] * n_in
    several = isinstance(out_shape, tuple)
    whole = pl.BlockSpec(memory_space=pltpu.VMEM)
    return pl.pallas_call(
        kernel,
        out_shape=out_shape,
        in_specs=specs,
        out_specs=(whole,) * len(out_shape) if several else whole,
        scratch_shapes=list(scratch),
        compiler_params=pltpu.CompilerParams(vmem_limit_bytes=limit),
    )


def _share(block, groups):
    copies = jnp.broadcast_to(block[None], (len(groups[0]),) + block.shape)
    return lax.all_to_all(copies, "patch", 0, 0, axis_index_groups=groups)


def on_device(latent, stale_hidden, input_proj, query_proj, key_proj, value_proj, output_proj):
    shape = jax.ShapeDtypeStruct
    latents = _share(latent.reshape(TOK, C), BRICKS)
    blocks = _call(pack_kernel, shape((NK, STATS + STAT_ROWS, LANES), BF), 2)(latents, stale_hidden)
    blocks = lax.all_to_all(blocks, "patch", 0, 0, axis_index_groups=SEATS)
    queries, own_queries, projected, hidden = _call(
        query_kernel,
        (shape((QROWS, C), BF), shape((TOK, C), BF), shape((TOK, C), F32), shape((TOK, C), BF)),
        4,
        scratch=(pltpu.VMEM((QROWS, C), F32), pltpu.VMEM((QROWS, C), BF)),
    )(latents, blocks, input_proj, query_proj)
    parts, own = _call(attend_kernel, (shape((NQ, TOK, WIDE), BF), shape((TOK, WIDE), BF)), 6)(
        queries, own_queries, hidden, blocks, key_proj, value_proj
    )
    parts = lax.all_to_all(parts, "patch", 0, 0, axis_index_groups=BRICKS)
    return _call(merge_kernel, (shape((1, TOK, C), BF), shape((TOK, C), BF)), 6)(
        parts, own, projected, hidden, latent, output_proj
    )


def solution(mesh):
    rows = P(("batch", "patch"), None)
    return jax.shard_map(
        on_device,
        mesh=mesh,
        in_specs=(P(("batch", "patch"), None, None), rows, P(), P(), P(), P(), P()),
        out_specs=(P(("batch", "patch"), None, None), rows),
        check_vma=False,
    )
```
